128 devices in a mesh: seq: 4 (over x_hi, core), pair: 8 (over z, x_lo), dp: 4 (over y).
Axes of the slice: x: 4 (x_hi: 2, x_lo: 2; x = x_hi * 2 + x_lo), y: 4, z: 4, core: 2. Of those that a mesh axis runs over, the one named last changes fastest.
Arguments:
- features: bfloat16 [4, 8, 2048, 1536], P('dp', 'pair', 'seq'), may hold values from -6 to 6
- conv_weight: bfloat16 [5, 1536, 1536], P(None, 'pair'), may hold values from -0.0625 to 0.0625
- conv_bias: float32 [1536], replicated, may hold values from -3 to 3
- species_table: float32 [2, 1536], replicated, may hold values from -3 to 3
- species_id: int32 [4, 8], P('dp'), may hold values from 0 to 1
- norm_gain: float32 [1536], replicated, may hold values from 0.4 to 1.6
- qkv_weight: bfloat16 [3, 1536, 1536], P(None, ('pair', 'dp')), may hold values from -5 to 5
- out_weight: bfloat16 [1536, 1536], P(('pair', 'dp')), may hold values from -0.15625 to 0.15625
- left_weight: bfloat16 [1536, 128], replicated, may hold values from -0.15625 to 0.15625
- right_weight: bfloat16 [1536, 128], replicated, may hold values from -0.15625 to 0.15625
- mix_weight: bfloat16 [128, 128], replicated, may hold values from -0.5 to 0.5
Outputs:
- seq_out: bfloat16 [4, 8, 1024, 1536], P('dp', 'pair', 'seq')
- pair_map: bfloat16 [4, 8, 64, 64, 128], P('dp', None, 'seq', 'pair')
The draws below stay inside these ranges and needn't reach their ends.
All inputs are finite; a program needn't handle non-finite values.
Results may differ from the reference program's by a relative error of at most 0.02.
Values may be sent and summed in bfloat16 or wider, within the bound.
A program may use at most 128 MiB of HBM per device.

```python
import math
import jax
import jax.numpy as jnp
from jax import lax

D = 1536
HEADS = 8
PC = 128
HEAD_DIM = 192
KW = 5
POOL = 16
SPECIES = 2
TOK_W = 1024
ROWS_W = 2048
PR = 64
GWIN = 8
GROUPS = 4


def draw_qkv_weight(key, part):
    key = jax.random.fold_in(key, 11)
    base = jnp.clip(jax.random.normal(key, (3, D, D), jnp.float32), -6.0, 6.0) / math.sqrt(D)
    return base.astype(jnp.bfloat16)


def with_ends(result, own_key, least, top_value):
    place = [jax.random.randint(jax.random.fold_in(own_key, axis), (), 0, length) for axis, length in enumerate(result.shape)]
    widest = result.shape.index(max(result.shape))
    next_to = place[:widest] + [(place[widest] + 1) % result.shape[widest]] + place[widest + 1:]
    return result.at[tuple(place)].set(least).at[tuple(next_to)].set(top_value)


def levels(stream_key, extent, split, low, high):
    factor_of, own = 1.0, jax.random.fold_in(stream_key, 6)
    for axis_at, shards_of in split:
        draws = jnp.exp(jax.random.uniform(jax.random.fold_in(own, axis_at), (shards_of,), jnp.float32, low / len(split), high / len(split)))
        factor_of = factor_of * jnp.repeat(draws, extent[axis_at] // shards_of).reshape([-1 if axis == axis_at else 1 for axis in range(len(extent))])
    return factor_of


def bell_draw(rng, shape, spread, most, pieces=(), dtype=jnp.bfloat16):
    factor_of = levels(rng, shape, pieces, -0.22, 0.18) if pieces else 1.0
    values = jax.random.normal(rng, shape, jnp.float32) * spread * factor_of
    return jnp.minimum(jnp.maximum(values, -most), most).astype(dtype)


def setup_inputs(seed: int = 0) -> dict:
    streams_of = jax.random.split(jax.random.key(seed), 12)
    features = bell_draw(streams_of[0], (GROUPS, GWIN, ROWS_W, D), 1.0, 6.0, ((0, 4), (1, 8), (2, 4)))
    conv_weight = bell_draw(streams_of[1], (KW, D, D), (KW * D) ** -0.5, 0.0625, ((1, 8),))
    conv_bias = bell_draw(streams_of[2], (D,), 0.4, 3.0, (), jnp.float32)
    species_table = bell_draw(streams_of[3], (SPECIES, D), 0.5, 3.0, (), jnp.float32)
    species_id = with_ends(jax.random.randint(streams_of[4], (GROUPS, GWIN), 0, SPECIES), jax.random.fold_in(streams_of[4], 1), 0, SPECIES - 1).astype(jnp.int32)
    norm_gain = jnp.clip(1.0 + 0.12 * jax.random.normal(streams_of[5], (D,), jnp.float32), 0.4, 1.6)
    qkv_weight = draw_qkv_weight(jax.random.fold_in(streams_of[11], 71), 0)
    out_weight = bell_draw(streams_of[7], (D, D), D ** -0.5, 0.15625, ((0, 32),))
    left_weight = bell_draw(streams_of[8], (D, PC), D ** -0.5, 0.15625)
    right_weight = bell_draw(streams_of[9], (D, PC), D ** -0.5, 0.15625)
    mix_weight = bell_draw(streams_of[10], (PC, PC), PC ** -0.5, 0.5)
    return dict(features=features, conv_weight=conv_weight, conv_bias=conv_bias, species_table=species_table, species_id=species_id, norm_gain=norm_gain, qkv_weight=qkv_weight, out_weight=out_weight, left_weight=left_weight, right_weight=right_weight, mix_weight=mix_weight)


def rms_scale(values):
    return values * lax.rsqrt(lax.optimization_barrier(jnp.mean(values * values, axis=-1, keepdims=True)) + 1e-05)

def one_window(feature_rows, species_row, conv_weight, conv_bias, norm_gain, qkv_weight, out_weight, left_weight, right_weight, mix_weight):
    margin = KW // 2
    padded = jnp.pad(feature_rows, ((margin, margin), (0, 0)))
    total = jnp.zeros((ROWS_W, D), jnp.float32) + conv_bias[None, :]
    for shift in range(KW):
        total = total + jnp.dot(padded[shift:shift + ROWS_W], conv_weight[shift].T, preferred_element_type=jnp.float32)
    active = jax.nn.gelu(total)
    pooled = lax.optimization_barrier(jnp.max(active.reshape(TOK_W, 2, D), axis=1))
    tokens = (pooled + species_row[None, :]).astype(jnp.bfloat16)
    normed = (rms_scale(tokens.astype(jnp.float32)) * norm_gain[None, :]).astype(jnp.bfloat16)
    query = jnp.dot(normed, qkv_weight[0].T, preferred_element_type=jnp.float32).astype(jnp.bfloat16)
    keys = jnp.dot(normed, qkv_weight[1].T, preferred_element_type=jnp.float32).astype(jnp.bfloat16)
    values = jnp.dot(normed, qkv_weight[2].T, preferred_element_type=jnp.float32).astype(jnp.bfloat16)
    query_h = query.astype(jnp.float32).reshape(TOK_W, HEADS, HEAD_DIM)
    keys_h = keys.astype(jnp.float32).reshape(TOK_W, HEADS, HEAD_DIM)
    values_h = values.astype(jnp.float32).reshape(TOK_W, HEADS, HEAD_DIM)
    scores = jnp.einsum('qhe,khe->hqk', query_h, keys_h) / math.sqrt(HEAD_DIM)
    probs = jax.nn.softmax(scores, axis=-1).astype(jnp.bfloat16)
    attended = jnp.einsum('hqk,khe->qhe', probs.astype(jnp.float32), values_h)
    attended = attended.astype(jnp.bfloat16).reshape(TOK_W, D)
    mixed = jnp.dot(attended, out_weight, preferred_element_type=jnp.float32)
    seq_out = (tokens.astype(jnp.float32) + mixed).astype(jnp.bfloat16)
    rows = lax.optimization_barrier(jnp.mean(seq_out.astype(jnp.float32).reshape(PR, POOL, D), axis=1))
    unit = rms_scale(rows).astype(jnp.bfloat16)
    left = jnp.dot(unit, left_weight, preferred_element_type=jnp.float32).astype(jnp.bfloat16)
    right = jnp.dot(unit, right_weight, preferred_element_type=jnp.float32).astype(jnp.bfloat16)
    outer = left[:, None, :] * right[None, :, :]
    pair_map = jnp.einsum('ijc,cd->ijd', outer.astype(jnp.float32), mix_weight.astype(jnp.float32))
    return (seq_out, pair_map.astype(jnp.bfloat16))

def reference(features, conv_weight, conv_bias, species_table, species_id, norm_gain, qkv_weight, out_weight, left_weight, right_weight, mix_weight):
    window_count = GROUPS * GWIN
    flat_features = features.reshape(window_count, ROWS_W, D)
    species_rows = species_table[species_id.reshape(window_count)]

    def per_window(packed):
        return one_window(packed[0], packed[1], conv_weight, conv_bias, norm_gain, qkv_weight, out_weight, left_weight, right_weight, mix_weight)
    seq_out, pair_map = lax.map(per_window, (flat_features, species_rows))
    return (seq_out.reshape(GROUPS, GWIN, TOK_W, D), pair_map.reshape(GROUPS, GWIN, PR, PR, PC))
```

```python
import math

import jax
import jax.numpy as jnp
from jax import lax
from jax.experimental import pallas as pl
from jax.experimental.pallas import tpu as pltpu
from jax.sharding import PartitionSpec as P

D = 1536
HEAD = 192
POOL = 16
SPECIES = 2
MESH = pl.DeviceIdType.MESH
BF = jnp.bfloat16
F32 = jnp.float32
HALF = 768
ROWS = 1120


def coords():
    s, p, y = lax.axis_index("seq"), lax.axis_index("pair"), lax.axis_index("dp")
    hi, c = lax.div(s, 2), lax.rem(s, 2)
    z, lo = lax.div(p, 2), lax.rem(p, 2)
    return s, p, y, hi, c, z, lo, 2 * hi + lo


def dev(x, y, z, c):
    return (2 * lax.div(x, 2) + c, 2 * z + lax.rem(x, 2), y)


def m4(v):
    return lax.rem(v + 4, 4)


def nt(a, b):
    return lax.dot_general(a, b, (((1,), (1,)), ((), ())), preferred_element_type=F32)


def nn(a, b):
    return lax.dot_general(a, b, (((1,), (0,)), ((), ())), preferred_element_type=F32)


def al(v, n):
    return pl.multiple_of(v, n)


class Sites:
    def __init__(self, ss, rs):
        self.ss, self.rs, self.n, self.all = ss, rs, 0, []

    def make(self, src, dst, device, pend=True):
        k = self.n
        self.n += 1
        cp = pltpu.make_async_remote_copy(
            src_ref=src, dst_ref=dst, send_sem=self.ss.at[k], recv_sem=self.rs.at[k],
            device_id=device, device_id_type=MESH,
        )
        if pend:
            self.all.append(cp)
        return cp

    def go(self, src, dst, device):
        cp = self.make(src, dst, device)
        cp.start()
        return cp


N_SITES = 128


def main_kernel(
    feat, cw_in, qkv_in, out_in, vec, lw, rw,
    seq_out, left_out, right_out,
    F, CW, acc, QT, AW, OW, TH, TA, TOK, NM, QH, AO, AT,
    ss, rs, ls,
):
    s, p, y, hi, c, z, lo, x = coords()
    xp, xm, x2 = m4(x + 1), m4(x - 1), m4(x + 2)
    sib = dev(x, y, z, 1 - c)
    st = Sites(ss, rs)

    barrier = pltpu.get_barrier_semaphore()
    peers = [sib]
    for xx in (xp, xm, x2):
        peers += [dev(xx, y, z, c), dev(xx, y, z, 1 - c)]
    for d in (1, -1):
        peers += [dev(x, m4(y + d), z, c), dev(x, y, m4(z + d), c)]
    for t in peers:
        pl.semaphore_signal(barrier, inc=1, device_id=t, device_id_type=MESH)

    lcopies = []

    def local(src, dst):
        cp = pltpu.make_async_copy(src, dst, ls.at[len(lcopies)])
        cp.start()
        lcopies.append(cp)
        return cp

    cols = pl.ds(al(c * HALF, 128), HALF)
    own_q = local(qkv_in, QT)
    own_f = local(feat, F.at[pl.ds(16, 512)])
    own_o = local(out_in.at[:, cols], OW.at[lo, z, y, :, cols])
    own_w = local(cw_in, CW.at[:, pl.ds(al(z * HEAD, 16), HEAD)])
    pl.semaphore_wait(barrier, len(peers))

    sgn = 1 - 2 * lax.rem(y + c, 2)
    zd, zs, zo = m4(z + sgn), m4(z - sgn), m4(z + 2)
    g = lax.rem(y + c, 2)
    r0 = c * 96
    to_z = dev(x, y, zd, c)

    def rows_of(slot, off, n):
        return pl.ds(al(slot * HEAD + r0 + off, 16), n)

    zA, zB, yA, yC, sb = {}, {}, {}, {}, {}

    def start_zA(t):
        zA[t] = st.go(cw_in.at[t, pl.ds(al(r0, 16), 96)], CW.at[t, rows_of(z, 0, 96)], to_z)

    def same(ref, device):
        return st.go(ref, ref, device)

    def pass_zA(t):
        zA[t].wait_recv()
        zB[t] = same(CW.at[t, rows_of(zs, 48 * g, 48)], to_z)
        yA[t] = [
            same(CW.at[t, rows_of(zs, 0, 48)], dev(x, m4(y + 1), z, c)),
            same(CW.at[t, rows_of(zs, 48, 48)], dev(x, m4(y - 1), z, c)),
        ]
        sb[t] = [same(CW.at[t, rows_of(zs, 0, 96)], sib)]

    def pass_zB(t):
        zB[t].wait_recv()
        yC[t] = same(CW.at[t, rows_of(zo, 48 * g, 48)], dev(x, m4(y + 1 - 2 * c), z, c))
        for cp in yA[t]:
            cp.wait_recv()
        sb[t].append(same(CW.at[t, rows_of(zd, 0, 96)], sib))

    def pass_yC(t):
        yC[t].wait_recv()
        sb[t].append(same(CW.at[t, rows_of(zo, 0, 96)], sib))

    start_zA(0)

    lastr, firstr = feat.at[pl.ds(496, 16)], feat.at[pl.ds(0, 16)]
    xn = m4(x + 2 * c)
    xq = m4(x + 2 * (1 - c))
    halo = [
        st.go(lastr, F.at[pl.ds(0, 16)], dev(xn, y, z, 1 - c)),
        st.go(firstr, F.at[pl.ds(528, 16)], dev(xq, y, z, 1 - c)),
        st.go(lastr, F.at[pl.ds(544, 16)], dev(m4(xn + 1), y, z, 1 - c)),
        st.go(firstr, F.at[pl.ds(1104, 16)], dev(m4(xq - 1), y, z, 1 - c)),
        st.go(feat.at[pl.ds(0, 272)], F.at[pl.ds(560, 272)], dev(xp, y, z, c)),
        st.go(feat.at[pl.ds(240, 272)], F.at[pl.ds(832, 272)], dev(xm, y, z, c)),
    ]
    start_zA(1)

    own_q.wait()
    for k in range(3):
        w = QT[k]
        QT[k] = jnp.concatenate(
            [w[:, (2 * b + a) * HEAD:(2 * b + a + 1) * HEAD] for a in range(2) for b in range(4)], axis=1
        )
    mine_q = AW.at[:, z, y, :, cols]
    swap_q = st.make(QT.at[:, :, cols], mine_q, dev(3 - x, y, z, c), pend=False)
    keep_q = pltpu.make_async_copy(QT.at[:, :, cols], mine_q, ls.at[4])

    @pl.when(hi == 0)
    def _():
        swap_q.start()
        keep_q.start()

    swap_o = st.go(out_in.at[:, cols], OW.at[lo, z, y, :, cols], dev(3 - x, y, z, c))

    acc[...] = jnp.zeros_like(acc)
    own_f.wait()
    own_w.wait()
    own_o.wait()

    def ready_features():
        for cp in halo:
            cp.wait_recv()
        sa = 2 * lax.div(xm, 2) + c
        sbk = 2 * lax.div(xp, 2) + c
        for cond, at in ((s == 0, 0), (s == 3, 528), (sa == 0, 544), (sbk == 3, 1104)):
            @pl.when(cond)
            def _(at=at):
                F[at:at + 16] = jnp.zeros((16, D), BF)

    def conv_tap(t):
        for cp in sb[t]:
            cp.wait_recv()

        def body(n, carry):
            at = al(n * 256, 256)
            out = nt(F[...], CW[t, pl.ds(at, 256), :])
            for j in range(2):
                acc[2 * n + j, 4 - t:4 - t + ROWS] += out[:, 128 * j:128 * j + 128]
            return carry

        lax.fori_loop(0, 3, body, 0)

    i0, k0 = (1 - c) * y + c * z, (1 - c) * z + c * y

    class Gather:
        def __init__(self, buf):
            self.buf = buf
            self.a2, self.b2 = {}, {}

        def ref(self, i, k, sub=None):
            zz, yy = (1 - c) * k + c * i, (1 - c) * i + c * k
            if sub is None:
                return self.buf.at[:, zz, yy, :, cols]
            return self.buf.at[:, zz, yy, :, pl.ds(al(c * HALF + 384 * sub, 128), 384)]

        def to(self, i, k):
            return dev(x, (1 - c) * i + c * k, (1 - c) * k + c * i, c)

        def second(self, j):
            i = m4(i0 + j)
            own = self.ref(i, k0)
            self.a2[j] = [same(own, self.to(i0, m4(k0 + d))) for d in (1, -1)]

        def second_pass(self, j):
            i = m4(i0 + j)
            self.a2[j][0].wait_recv()
            self.b2[j] = [same(self.ref(i, m4(k0 - 1), 0), self.to(i0, m4(k0 + 1)))]
            self.a2[j][1].wait_recv()
            self.b2[j].append(same(self.ref(i, m4(k0 + 1), 1), self.to(i0, m4(k0 - 1))))

        def p0(self):
            own = self.ref(i0, k0)
            self.a1 = [same(own, self.to(m4(i0 + d), k0)) for d in (1, -1)]
            self.second(0)

        def p1(self):
            self.a1[0].wait_recv()
            self.b1 = [same(self.ref(m4(i0 - 1), k0, 0), self.to(m4(i0 + 1), k0))]
            self.second(-1)
            self.a1[1].wait_recv()
            self.b1.append(same(self.ref(m4(i0 + 1), k0, 1), self.to(m4(i0 - 1), k0)))
            self.second(1)

        def p2(self):
            self.second_pass(0)
            for cp in self.b1:
                cp.wait_recv()
            self.second(2)

        def p3(self):
            self.second_pass(-1)
            self.second_pass(1)

        def p4(self):
            self.second_pass(2)

        def p5(self):
            for j in (0, -1, 1, 2):
                for cp in self.b2[j]:
                    cp.wait_recv()

    gq, go = Gather(AW), Gather(OW)

    order = [0, 1, 2, 3, 4]
    for step in range(7):
        if step < 5:
            pass_zA(order[step])
            if step + 2 < 5:
                start_zA(order[step + 2])
        if step == 4:
            @pl.when(hi == 0)
            def _():
                keep_q.wait()

            @pl.when(hi == 1)
            def _():
                swap_q.wait_recv()
            gq.p0()
        if 1 <= step < 6:
            pass_zB(order[step - 1])
        if step == 5:
            gq.p1()
        if step >= 2:
            if step == 2:
                ready_features()
            pass_yC(order[step - 2])
            conv_tap(order[step - 2])

    gq.p2()

    bias = vec[lo]
    wo = 2 * z + (1 - lo)

    def tokens(at, window):
        species = vec[2 * (2 + window) + lo]
        cut = []
        for j in range(6):
            lanes = slice(128 * j, 128 * j + 128)
            even = jax.nn.gelu(acc[j, pl.ds(at, 128, stride=2), :] + bias[:, lanes])
            odd = jax.nn.gelu(acc[j, pl.ds(at + 1, 128, stride=2), :] + bias[:, lanes])
            cut.append((jnp.maximum(even, odd) + species[:, lanes]).astype(BF))
        return jnp.concatenate(cut, axis=1)

    TA[0:128] = tokens(562, wo)
    TA[128:256] = tokens(850, wo)
    a0 = (2 * lax.div(xm, 2) + c) * 256
    b0 = (2 * lax.div(xp, 2) + c) * 256 + 128
    ta, tb = TH.at[lo, pl.ds(al(a0, 128), 128)], TH.at[lo, pl.ds(al(b0, 128), 128)]
    cross = []
    for xx in (xp, xm):
        cross += [
            st.go(TA.at[pl.ds(0, 128)], ta, dev(xx, y, z, c)),
            st.go(TA.at[pl.ds(128, 128)], tb, dev(xx, y, z, c)),
        ]
    TH[lo, pl.ds(al(s * 256, 256), 128)] = tokens(18, p)
    TH[lo, pl.ds(al(s * 256 + 128, 128), 128)] = tokens(274, p)
    s2 = 2 * (1 - hi) + c
    blk = pl.ds(al(s * 256, 256), 256)
    blk2 = pl.ds(al(s2 * 256, 256), 256)
    far = same(TH.at[lo, blk], dev(x2, y, z, c))
    near = [same(TH.at[lo, blk], sib)]

    gq.p3()
    for cp in cross:
        cp.wait_recv()
    near.append(same(TH.at[1 - lo, blk], sib))
    far.wait_recv()
    near.append(same(TH.at[lo, blk2], sib))
    near.append(same(TH.at[1 - lo, blk2], sib))
    gq.p4()
    gq.p5()
    other = pl.ds(al(2 * (1 - c), 2), 2)
    sq = same(AW.at[:, other, :, :, cols], sib)
    swap_o.wait_recv()
    go.p0()

    def norm(block):
        at = pl.ds(al(block * 256, 256), 256)
        h0 = TH[0, at].astype(F32)
        h1 = TH[1, at].astype(F32)
        ms = (jnp.sum(h0 * h0, axis=1, keepdims=True) + jnp.sum(h1 * h1, axis=1, keepdims=True)) / D
        r = lax.rsqrt(ms + 1e-05)
        NM[at, 0:HALF] = (h0 * r * vec[2]).astype(BF)
        NM[at, HALF:D] = (h1 * r * vec[3]).astype(BF)

    norm(s)
    norm(s2)
    hs = [TH[a, blk] for a in range(2)]
    TOK[...] = jnp.concatenate([hs[a][:, b * HEAD:(b + 1) * HEAD] for b in range(4) for a in range(2)], axis=1)
    go.p1()
    for cp in near:
        cp.wait_recv()
    norm(2 * hi + 1 - c)
    norm(2 * (1 - hi) + 1 - c)
    go.p2()
    sq.wait_recv()

    for part in range(3):
        w = AW[part, pl.ds(al(2 * c, 2), 2)].reshape(2 * HEAD, D)
        res = nt(NM[...], w).astype(BF)
        for h in range(2):
            QH[part, h] = res[:, h * HEAD:(h + 1) * HEAD]
    go.p3()

    scale = 1.0 / math.sqrt(HEAD)
    lop = lax.rem(lo + hi, 2)
    my_cols = pl.ds(al((2 * lop + c) * 384, 128), 384)
    back = []
    dests = [(1 - hi, c, x2, c), (1 - hi, 1 - c, x2, 1 - c), (hi, 1 - c, x, 1 - c), (hi, c, None, None)]
    for d, (dhi, dc, dx, dcc) in enumerate(dests):
        at = pl.ds(al((2 * dhi + dc) * 256, 256), 256)
        for h in range(2):
            sc = nt(QH[0, h, at], QH[1, h]) * scale
            e = jnp.exp(sc - jnp.max(sc, axis=1, keepdims=True))
            inv = 1.0 / jnp.sum(e, axis=1, keepdims=True)
            AO[d, h] = (nn(e.astype(BF), QH[2, h]) * inv).astype(BF)
        both = jnp.concatenate([AO[d, 0], AO[d, 1]], axis=1)
        if dx is None:
            AT[:, my_cols] = both
        else:
            NM[d * 256:(d + 1) * 256, 0:384] = both
            back.append(st.go(NM.at[pl.ds(d * 256, 256), pl.ds(0, 384)], AT.at[:, my_cols], dev(dx, y, z, dcc)))
        if d == 1:
            go.p4()
            go.p5()
            so = same(OW.at[:, :, :, :, cols], sib)

    so.wait_recv()
    for cp in back:
        cp.wait_recv()

    def out_body(n, carry):
        at = pl.ds(al(n * 256, 256), 256)
        mixed = nn(AT[...], OW[:, :, :, :, at].reshape(D, 256))
        seq_out[:, at] = (TOK[:, at].astype(F32) + mixed).astype(BF)
        return carry

    lax.fori_loop(0, 6, out_body, 0)

    rows = jnp.sum(seq_out[...].astype(F32).reshape(16, POOL, D), axis=1) * (1.0 / POOL)
    unit = (rows * lax.rsqrt(jnp.mean(rows * rows, axis=1, keepdims=True) + 1e-05)).astype(BF)
    left_out[...] = nn(unit, lw[...]).astype(BF)
    right_out[...] = nn(unit, rw[...]).astype(BF).astype(F32)

    for cp in st.all:
        cp.wait_send()

    @pl.when(hi == 0)
    def _():
        swap_q.wait_send()


def pair_kernel(left, right, mix, out, L, R, ssl, rsl, ssr, rsr):
    s, p, y, hi, c, z, lo, x = coords()
    barrier = pltpu.get_barrier_semaphore()
    inside = lax.div(p, 2) == s
    for d in range(1, 8):
        pl.semaphore_signal(barrier, inc=1, device_id=(s, lax.rem(p + d, 8), y), device_id_type=MESH)
    for w in range(8):
        @pl.when(jnp.logical_not(jnp.logical_and(inside, p == w)))
        def _(w=w):
            pl.semaphore_signal(barrier, inc=1, device_id=(lax.div(p, 2), w, y), device_id_type=MESH)
    pl.semaphore_wait(barrier, 15 - inside.astype(jnp.int32))

    lefts = []
    for d in range(1, 8):
        cp = pltpu.make_async_remote_copy(
            src_ref=left, dst_ref=L.at[p], send_sem=ssl.at[d], recv_sem=rsl.at[d],
            device_id=(s, lax.rem(p + d, 8), y), device_id_type=MESH,
        )
        cp.start()
        lefts.append(cp)
    L[p] = left[...]

    def right_copy(q, half):
        return pltpu.make_async_remote_copy(
            src_ref=right.at[pl.ds(8 * half, 8)], dst_ref=R.at[p], send_sem=ssr.at[2 * q + half],
            recv_sem=rsr.at[p], device_id=(q, 2 * s + half, y), device_id_type=MESH,
        )

    for q in range(4):
        for half in range(2):
            me = jnp.logical_and(p == 2 * s + half, q == s)

            @pl.when(jnp.logical_not(me))
            def _(q=q, half=half):
                right_copy(q, half).start()

            @pl.when(me)
            def _(half=half):
                R[p] = right[8 * half:8 * half + 8, :]

    for cp in lefts:
        cp.wait_recv()
    for w in range(8):
        @pl.when(jnp.logical_not(jnp.logical_and(inside, p == w)))
        def _(w=w):
            pltpu.make_async_remote_copy(
                src_ref=right.at[pl.ds(0, 8)], dst_ref=R.at[w], send_sem=ssr.at[0],
                recv_sem=rsr.at[w], device_id=(s, p, y), device_id_type=MESH,
            ).wait_recv()

    outer = L[...].astype(F32)[:, :, None, :] * R[...][:, None, :, :]
    out[...] = nn(outer.reshape(1024, 128).astype(BF), mix[...]).astype(BF)
    for cp in lefts:
        cp.wait_send()
    for q in range(4):
        for half in range(2):
            @pl.when(jnp.logical_not(jnp.logical_and(p == 2 * s + half, q == s)))
            def _(q=q, half=half):
                right_copy(q, half).wait_send()


def local(
    features, conv_weight, conv_bias, species_table, species_id, norm_gain,
    qkv_weight, out_weight, left_weight, right_weight, mix_weight,
):
    species_rows = jnp.where(species_id[0][:, None] == 0, species_table[0][None, :], species_table[1][None, :])
    vec = jnp.concatenate([conv_bias[None], norm_gain[None], species_rows], axis=0)
    vec = vec.reshape(10, 4, 2, HEAD).transpose(0, 2, 1, 3).reshape(20, 1, HALF)
    any_ = pl.BlockSpec(memory_space=pl.ANY)
    vm = pl.BlockSpec(memory_space=pltpu.VMEM)
    seq_out, left, right = pl.pallas_call(
        main_kernel,
        out_shape=(
            jax.ShapeDtypeStruct((256, D), BF),
            jax.ShapeDtypeStruct((16, 128), BF),
            jax.ShapeDtypeStruct((16, 128), F32),
        ),
        in_specs=[any_, any_, any_, any_, vm, vm, vm],
        out_specs=(vm, vm, vm),
        scratch_shapes=[
            pltpu.VMEM((ROWS, D), BF),
            pltpu.VMEM((5, HALF, D), BF),
            pltpu.VMEM((6, ROWS + 8, 128), F32),
            pltpu.VMEM((3, 48, D), BF),
            pltpu.VMEM((3, 4, 4, 48, D), BF),
            pltpu.VMEM((2, 4, 4, 48, D), BF),
            pltpu.VMEM((2, 1024, HALF), BF),
            pltpu.VMEM((256, HALF), BF),
            pltpu.VMEM((256, D), BF),
            pltpu.VMEM((1024, D), BF),
            pltpu.VMEM((3, 2, 1024, HEAD), BF),
            pltpu.VMEM((4, 2, 256, HEAD), BF),
            pltpu.VMEM((256, D), BF),
            pltpu.SemaphoreType.DMA((N_SITES,)),
            pltpu.SemaphoreType.DMA((N_SITES,)),
            pltpu.SemaphoreType.DMA((5,)),
        ],
        compiler_params=pltpu.CompilerParams(
            collective_id=0, has_side_effects=True, vmem_limit_bytes=62 * 2**20
        ),
        name="window",
    )(features.reshape(512, D), conv_weight, qkv_weight, out_weight, vec, left_weight, right_weight)
    pair_map = pl.pallas_call(
        pair_kernel,
        out_shape=jax.ShapeDtypeStruct((1024, 128), BF),
        in_specs=[vm, vm, vm],
        out_specs=vm,
        scratch_shapes=[
            pltpu.VMEM((8, 16, 128), BF),
            pltpu.VMEM((8, 8, 128), F32),
            pltpu.SemaphoreType.DMA((8,)),
            pltpu.SemaphoreType.DMA((8,)),
            pltpu.SemaphoreType.DMA((8,)),
            pltpu.SemaphoreType.DMA((8,)),
        ],
        compiler_params=pltpu.CompilerParams(collective_id=1, has_side_effects=True),
        name="pairs",
    )(left, right, mix_weight)
    return seq_out[None, None], pair_map.reshape(1, 8, 16, 8, 128)


def solution(mesh):
    return jax.shard_map(
        local,
        mesh=mesh,
        in_specs=(
            P("dp", "pair", "seq", None),
            P(None, "pair", None),
            P(),
            P(),
            P("dp", None),
            P(),
            P(None, ("pair", "dp"), None),
            P(("pair", "dp"), None),
            P(),
            P(),
            P(),
        ),
        out_specs=(P("dp", "pair", "seq", None), P("dp", None, "seq", "pair", None)),
        check_vma=False,
    )
```

```python
import math

import jax
import jax.numpy as jnp
from jax import lax
from jax.experimental import pallas as pl
from jax.experimental.pallas import tpu as pltpu
from jax.sharding import PartitionSpec as P

D = 1536
HEAD = 192
POOL = 16
SPECIES = 2
MESH = pl.DeviceIdType.MESH
BF = jnp.bfloat16
F32 = jnp.float32
HALF = 768
ROWS = 1120


def coords():
    s, p, y = lax.axis_index("seq"), lax.axis_index("pair"), lax.axis_index("dp")
    hi, c = lax.div(s, 2), lax.rem(s, 2)
    z, lo = lax.div(p, 2), lax.rem(p, 2)
    return s, p, y, hi, c, z, lo, 2 * hi + lo


def dev(x, y, z, c):
    return (2 * lax.div(x, 2) + c, 2 * z + lax.rem(x, 2), y)


def m4(v):
    return lax.rem(v + 4, 4)


def nt(a, b):
    return lax.dot_general(a, b, (((1,), (1,)), ((), ())), preferred_element_type=F32)


def nn(a, b):
    return lax.dot_general(a, b, (((1,), (0,)), ((), ())), preferred_element_type=F32)


def al(v, n):
    return pl.multiple_of(v, n)


class Sites:
    def __init__(self, ss, rs):
        self.ss, self.rs, self.n, self.all = ss, rs, 0, []

    def make(self, src, dst, device, pend=True):
        k = self.n
        self.n += 1
        cp = pltpu.make_async_remote_copy(
            src_ref=src, dst_ref=dst, send_sem=self.ss.at[k], recv_sem=self.rs.at[k],
            device_id=device, device_id_type=MESH,
        )
        if pend:
            self.all.append(cp)
        return cp

    def go(self, src, dst, device):
        cp = self.make(src, dst, device)
        cp.start()
        return cp


N_SITES = 160
CHUNKS = [(n, lo, hi) for n in range(3) for lo, hi in ((0, 3), (3, 5))]


def by_window(v):
    return jnp.concatenate(
        [v[:, at:at + 64] for a in range(2) for n in range(3) for at in [(2 * b + a) * HEAD + n * 64 for b in range(4)]],
        axis=1,
    )


def main_kernel(
    feat, cw_in, qkv_in, out_in, bias_in, gain_in, table_in, id_in, lw, rw,
    seq_out, left_out, right_out,
    F, CW, acc, QT, AW, OW, TH, TA, TOK, NM, QH, AO, AT, VEC,
    ss, rs, ls,
):
    s, p, y, hi, c, z, lo, x = coords()
    xp, xm, x2 = m4(x + 1), m4(x - 1), m4(x + 2)
    sib = dev(x, y, z, 1 - c)
    st = Sites(ss, rs)

    barrier = pltpu.get_barrier_semaphore()
    peers = [sib]
    for xx in (xp, xm, x2):
        peers += [dev(xx, y, z, c), dev(xx, y, z, 1 - c)]
    for d in (1, -1):
        peers += [dev(x, m4(y + d), z, c), dev(x, y, m4(z + d), c)]
    for t in peers:
        pl.semaphore_signal(barrier, inc=1, device_id=t, device_id_type=MESH)

    lcopies = []

    def local(src, dst):
        cp = pltpu.make_async_copy(src, dst, ls.at[len(lcopies)])
        cp.start()
        lcopies.append(cp)
        return cp

    cols = pl.ds(al(c * HALF, 128), HALF)
    own_q = local(qkv_in, QT)
    own_f = local(feat, F.at[pl.ds(16, 512)])
    own_o = local(out_in.at[:, cols], OW.at[lo, z, y, :, cols])
    own_w = [local(cw_in.at[:, pl.ds(64 * n, 64)], CW.at[n, :, pl.ds(al(z * 64, 16), 64)]) for n in range(3)]
    pl.semaphore_wait(barrier, len(peers))

    sgn = 1 - 2 * lax.rem(y + c, 2)
    zd, zs, zo = m4(z + sgn), m4(z - sgn), m4(z + 2)
    g = lax.rem(y + c, 2)
    to_z = dev(x, y, zd, c)

    def part(k, slot, off, rows):
        n, t0, t1 = CHUNKS[k]
        return CW.at[n, pl.ds(t0, t1 - t0), pl.ds(al(slot * 64 + c * 32 + off, 16), rows)]

    zA, zB, yA, yC, sb = {}, {}, {}, {}, {}

    def same(ref, device):
        return st.go(ref, ref, device)

    def start_zA(k):
        if k < len(CHUNKS):
            n, t0, t1 = CHUNKS[k]
            src = cw_in.at[pl.ds(t0, t1 - t0), pl.ds(al(n * 64 + c * 32, 16), 32)]
            zA[k] = st.go(src, part(k, z, 0, 32), to_z)

    def pass_zA(k):
        zA[k].wait_recv()
        zB[k] = same(part(k, zs, 16 * g, 16), to_z)
        yA[k] = [
            same(part(k, zs, 0, 16), dev(x, m4(y + 1), z, c)),
            same(part(k, zs, 16, 16), dev(x, m4(y - 1), z, c)),
        ]
        sb[k] = [same(part(k, zs, 0, 32), sib)]
        start_zA(k + 3)

    def pass_zB(k):
        zB[k].wait_recv()
        yC[k] = same(part(k, zo, 16 * g, 16), dev(x, m4(y + 1 - 2 * c), z, c))
        for cp in yA[k]:
            cp.wait_recv()
        sb[k].append(same(part(k, zd, 0, 32), sib))

    def pass_yC(k):
        yC[k].wait_recv()
        sb[k].append(same(part(k, zo, 0, 32), sib))

    start_zA(0)

    lastr, firstr = feat.at[pl.ds(496, 16)], feat.at[pl.ds(0, 16)]
    xn = m4(x + 2 * c)
    xq = m4(x + 2 * (1 - c))
    halo = [
        st.go(lastr, F.at[pl.ds(0, 16)], dev(xn, y, z, 1 - c)),
        st.go(firstr, F.at[pl.ds(528, 16)], dev(xq, y, z, 1 - c)),
        st.go(lastr, F.at[pl.ds(544, 16)], dev(m4(xn + 1), y, z, 1 - c)),
        st.go(firstr, F.at[pl.ds(1104, 16)], dev(m4(xq - 1), y, z, 1 - c)),
        st.go(feat.at[pl.ds(0, 272)], F.at[pl.ds(560, 272)], dev(xp, y, z, c)),
        st.go(feat.at[pl.ds(240, 272)], F.at[pl.ds(832, 272)], dev(xm, y, z, c)),
    ]
    start_zA(1)
    start_zA(2)

    VEC[0:1] = by_window(bias_in[...])
    VEC[1:2] = by_window(gain_in[...])
    VEC[2:4] = by_window(table_in[...])
    own_q.wait()
    for k in range(3):
        QT[k] = by_window(QT[k])
    mine_q = AW.at[:, z, y, :, cols]
    swap_q = st.make(QT.at[:, :, cols], mine_q, dev(3 - x, y, z, c), pend=False)
    keep_q = pltpu.make_async_copy(QT.at[:, :, cols], mine_q, ls.at[6])
    swap_o = st.make(out_in.at[:, cols], OW.at[lo, z, y, :, cols], dev(3 - x, y, z, c))

    acc[...] = jnp.zeros_like(acc)
    own_f.wait()
    own_o.wait()
    for cp in own_w:
        cp.wait()

    def ready_features():
        for cp in halo:
            cp.wait_recv()
        sa = 2 * lax.div(xm, 2) + c
        sbk = 2 * lax.div(xp, 2) + c
        for cond, at in ((s == 0, 0), (s == 3, 528), (sa == 0, 544), (sbk == 3, 1104)):
            @pl.when(cond)
            def _(at=at):
                F[at:at + 16] = jnp.zeros((16, D), BF)

    def start_swap():
        @pl.when(hi == 0)
        def _():
            swap_q.start()
            keep_q.start()
        swap_o.start()

    def wait_swap():
        @pl.when(hi == 0)
        def _():
            keep_q.wait()

        @pl.when(hi == 1)
        def _():
            swap_q.wait_recv()

    def conv_ready(n):
        for k in (2 * n, 2 * n + 1):
            for cp in sb[k]:
                cp.wait_recv()

    def conv_tap(n, t):
        out = nt(F[...], CW[n, t])
        for j in range(2):
            acc[2 * n + j, 4 - t:4 - t + ROWS] += out[:, 128 * j:128 * j + 128]

    i0, k0 = (1 - c) * y + c * z, (1 - c) * z + c * y

    class Gather:
        def __init__(self, buf):
            self.buf = buf
            self.a2, self.b2 = {}, {}

        def ref(self, i, k, sub=None):
            zz, yy = (1 - c) * k + c * i, (1 - c) * i + c * k
            if sub is None:
                return self.buf.at[:, zz, yy, :, cols]
            return self.buf.at[:, zz, yy, :, pl.ds(al(c * HALF + 384 * sub, 128), 384)]

        def to(self, i, k):
            return dev(x, (1 - c) * i + c * k, (1 - c) * k + c * i, c)

        def second(self, j):
            i = m4(i0 + j)
            own = self.ref(i, k0)
            self.a2[j] = [same(own, self.to(i0, m4(k0 + d))) for d in (1, -1)]

        def second_pass(self, j):
            i = m4(i0 + j)
            self.a2[j][0].wait_recv()
            self.b2[j] = [same(self.ref(i, m4(k0 - 1), 0), self.to(i0, m4(k0 + 1)))]
            self.a2[j][1].wait_recv()
            self.b2[j].append(same(self.ref(i, m4(k0 + 1), 1), self.to(i0, m4(k0 - 1))))

        def p0(self):
            own = self.ref(i0, k0)
            self.a1 = [same(own, self.to(m4(i0 + d), k0)) for d in (1, -1)]
            self.second(0)

        def p1(self):
            self.a1[0].wait_recv()
            self.b1 = [same(self.ref(m4(i0 - 1), k0, 0), self.to(m4(i0 + 1), k0))]
            self.second(-1)
            self.a1[1].wait_recv()
            self.b1.append(same(self.ref(m4(i0 + 1), k0, 1), self.to(m4(i0 - 1), k0)))
            self.second(1)

        def p2(self):
            self.second_pass(0)
            for cp in self.b1:
                cp.wait_recv()
            self.second(2)

        def p3(self):
            self.second_pass(-1)
            self.second_pass(1)

        def p4(self):
            self.second_pass(2)

        def p5(self):
            for j in (0, -1, 1, 2):
                for cp in self.b2[j]:
                    cp.wait_recv()

    gq, go = Gather(AW), Gather(OW)

    s2 = 2 * (1 - hi) + c
    blk = pl.ds(al(s * 256, 256), 256)
    blk2 = pl.ds(al(s2 * 256, 256), 256)
    a0 = (2 * lax.div(xm, 2) + c) * 256
    b0 = (2 * lax.div(xp, 2) + c) * 256 + 128
    ids = id_in[...]
    lane = lax.broadcasted_iota(jnp.int32, (1, 8), 1)

    def piece(row, n):
        both = [VEC[row:row + 1, a * HALF + n * 256:a * HALF + n * 256 + 256] for a in range(2)]
        return jnp.where(jnp.full((1, 256), lo, jnp.int32) == 0, both[0], both[1])

    def tokens(at, window, n):
        kind = jnp.sum(jnp.where(lane == window, ids, 0), axis=1, keepdims=True)
        species = jnp.where(jnp.broadcast_to(kind, (1, 256)) == 0, piece(2, n), piece(3, n))
        bias = piece(0, n)
        cut = []
        for j in range(2):
            lanes = slice(128 * j, 128 * j + 128)
            even = jax.nn.gelu(acc[2 * n + j, pl.ds(at, 128, stride=2), :] + bias[:, lanes])
            odd = jax.nn.gelu(acc[2 * n + j, pl.ds(at + 1, 128, stride=2), :] + bias[:, lanes])
            cut.append((jnp.maximum(even, odd) + species[:, lanes]).astype(BF))
        return jnp.concatenate(cut, axis=1)

    cross, far, near = {}, {}, {}

    def send_tokens(n):
        wo = 2 * z + (1 - lo)
        TA[n, 0:128] = tokens(562, wo, n)
        TA[n, 128:256] = tokens(850, wo, n)
        ta, tb = TH.at[lo, n, pl.ds(al(a0, 128), 128)], TH.at[lo, n, pl.ds(al(b0, 128), 128)]
        cross[n] = []
        for xx in (xp, xm):
            cross[n] += [
                st.go(TA.at[n, pl.ds(0, 128)], ta, dev(xx, y, z, c)),
                st.go(TA.at[n, pl.ds(128, 128)], tb, dev(xx, y, z, c)),
            ]
        TH[lo, n, pl.ds(al(s * 256, 256), 128)] = tokens(18, p, n)
        TH[lo, n, pl.ds(al(s * 256 + 128, 128), 128)] = tokens(274, p, n)
        far[n] = same(TH.at[lo, n, blk], dev(x2, y, z, c))
        near[n] = [same(TH.at[lo, n, blk], sib)]

    def pass_tokens(n):
        for cp in cross[n]:
            cp.wait_recv()
        near[n].append(same(TH.at[1 - lo, n, blk], sib))
        near[n].append(same(TH.at[1 - lo, n, blk2], sib))
        far[n].wait_recv()
        near[n].append(same(TH.at[lo, n, blk2], sib))

    def norm(block):
        at = pl.ds(al(block * 256, 256), 256)
        ms = 0.0
        for a in range(2):
            for n in range(3):
                h = TH[a, n, at].astype(F32)
                ms = ms + jnp.sum(h * h, axis=1, keepdims=True)
        r = lax.rsqrt(ms / D + 1e-05)
        for a in range(2):
            for n in range(3):
                lanes = slice(a * HALF + n * 256, a * HALF + n * 256 + 256)
                NM[at, lanes] = (TH[a, n, at].astype(F32) * r * VEC[1:2, lanes]).astype(BF)

    pass_zA(0)
    pass_zA(1)
    pass_zB(0)
    pass_zA(2)
    pass_zB(1)
    pass_yC(0)
    pass_zA(3)
    pass_zB(2)
    pass_yC(1)
    ready_features()
    start_swap()
    conv_ready(0)
    conv_tap(0, 0)
    conv_tap(0, 1)
    pass_zA(4)
    pass_zB(3)
    pass_yC(2)
    conv_tap(0, 2)
    conv_tap(0, 3)
    conv_tap(0, 4)
    pass_zA(5)
    pass_zB(4)
    pass_yC(3)
    send_tokens(0)
    pass_zB(5)
    pass_yC(4)
    wait_swap()
    gq.p0()
    conv_ready(1)
    conv_tap(1, 0)
    conv_tap(1, 1)
    pass_yC(5)
    conv_tap(1, 2)
    conv_tap(1, 3)
    gq.p1()
    conv_tap(1, 4)
    send_tokens(1)
    conv_ready(2)
    conv_tap(2, 0)
    conv_tap(2, 1)
    gq.p2()
    conv_tap(2, 2)
    conv_tap(2, 3)
    pass_tokens(0)
    conv_tap(2, 4)
    send_tokens(2)
    gq.p3()
    pass_tokens(1)
    gq.p4()
    swap_o.wait_recv()
    go.p0()
    pass_tokens(2)
    norm(s)
    norm(s2)
    hs = {(a, n): TH[a, n, blk] for a in range(2) for n in range(3)}
    TOK[...] = jnp.concatenate(
        [hs[a, n][:, b * 64:(b + 1) * 64] for b in range(4) for a in range(2) for n in range(3)], axis=1
    )
    gq.p5()
    other = pl.ds(al(2 * (1 - c), 2), 2)
    sq = same(AW.at[:, other, :, :, cols], sib)
    go.p1()
    for n in range(3):
        for cp in near[n]:
            cp.wait_recv()
    norm(2 * hi + 1 - c)
    norm(2 * (1 - hi) + 1 - c)
    go.p2()
    sq.wait_recv()

    for k in range(3):
        w = AW[k, pl.ds(al(2 * c, 2), 2)].reshape(2 * HEAD, D)
        res = nt(NM[...], w).astype(BF)
        for h in range(2):
            QH[k, h] = res[:, h * HEAD:(h + 1) * HEAD]
    go.p3()

    scale = 1.0 / math.sqrt(HEAD)
    lop = lax.rem(lo + hi, 2)
    my_cols = pl.ds(al((2 * lop + c) * 384, 128), 384)
    back = []
    dests = [(1 - hi, c, x2, c), (1 - hi, 1 - c, x2, 1 - c), (hi, 1 - c, x, 1 - c), (hi, c, None, None)]
    for d, (dhi, dc, dx, dcc) in enumerate(dests):
        at = pl.ds(al((2 * dhi + dc) * 256, 256), 256)
        for h in range(2):
            sc = nt(QH[0, h, at], QH[1, h]) * scale
            e = jnp.exp(sc - jnp.max(sc, axis=1, keepdims=True))
            inv = 1.0 / jnp.sum(e, axis=1, keepdims=True)
            AO[d, h] = (nn(e.astype(BF), QH[2, h]) * inv).astype(BF)
        both = jnp.concatenate([AO[d, 0], AO[d, 1]], axis=1)
        if dx is None:
            AT[:, my_cols] = both
        else:
            NM[d * 256:(d + 1) * 256, 0:384] = both
            back.append(st.go(NM.at[pl.ds(d * 256, 256), pl.ds(0, 384)], AT.at[:, my_cols], dev(dx, y, z, dcc)))
        if d == 0:
            go.p4()
        if d == 1:
            go.p5()
            so = same(OW.at[:, :, :, :, cols], sib)

    so.wait_recv()
    for cp in back:
        cp.wait_recv()

    def out_body(n, carry):
        at = pl.ds(al(n * 256, 256), 256)
        mixed = nn(AT[...], OW[:, :, :, :, at].reshape(D, 256))
        seq_out[:, at] = (TOK[:, at].astype(F32) + mixed).astype(BF)
        return carry

    lax.fori_loop(0, 6, out_body, 0)

    rows = jnp.sum(seq_out[...].astype(F32).reshape(16, POOL, D), axis=1) * (1.0 / POOL)
    unit = (rows * lax.rsqrt(jnp.mean(rows * rows, axis=1, keepdims=True) + 1e-05)).astype(BF)
    left_out[...] = nn(unit, lw[...]).astype(BF)
    right_out[...] = nn(unit, rw[...]).astype(BF).astype(F32)

    for cp in st.all:
        cp.wait_send()

    @pl.when(hi == 0)
    def _():
        swap_q.wait_send()


def pair_kernel(left, right, mix, out, L, R, ssl, rsl, ssr, rsr):
    s, p, y, hi, c, z, lo, x = coords()
    barrier = pltpu.get_barrier_semaphore()
    inside = lax.div(p, 2) == s
    for d in range(1, 8):
        pl.semaphore_signal(barrier, inc=1, device_id=(s, lax.rem(p + d, 8), y), device_id_type=MESH)
    for w in range(8):
        @pl.when(jnp.logical_not(jnp.logical_and(inside, p == w)))
        def _(w=w):
            pl.semaphore_signal(barrier, inc=1, device_id=(lax.div(p, 2), w, y), device_id_type=MESH)
    pl.semaphore_wait(barrier, 15 - inside.astype(jnp.int32))

    lefts = []
    for d in range(1, 8):
        cp = pltpu.make_async_remote_copy(
            src_ref=left, dst_ref=L.at[p], send_sem=ssl.at[d], recv_sem=rsl.at[d],
            device_id=(s, lax.rem(p + d, 8), y), device_id_type=MESH,
        )
        cp.start()
        lefts.append(cp)
    L[p] = left[...]

    def right_copy(q, half):
        return pltpu.make_async_remote_copy(
            src_ref=right.at[pl.ds(8 * half, 8)], dst_ref=R.at[p], send_sem=ssr.at[2 * q + half],
            recv_sem=rsr.at[p], device_id=(q, 2 * s + half, y), device_id_type=MESH,
        )

    for q in range(4):
        for half in range(2):
            me = jnp.logical_and(p == 2 * s + half, q == s)

            @pl.when(jnp.logical_not(me))
            def _(q=q, half=half):
                right_copy(q, half).start()

            @pl.when(me)
            def _(half=half):
                R[p] = right[8 * half:8 * half + 8, :]

    for cp in lefts:
        cp.wait_recv()
    for w in range(8):
        @pl.when(jnp.logical_not(jnp.logical_and(inside, p == w)))
        def _(w=w):
            pltpu.make_async_remote_copy(
                src_ref=right.at[pl.ds(0, 8)], dst_ref=R.at[w], send_sem=ssr.at[0],
                recv_sem=rsr.at[w], device_id=(s, p, y), device_id_type=MESH,
            ).wait_recv()

    outer = L[...].astype(F32)[:, :, None, :] * R[...][:, None, :, :]
    out[...] = nn(outer.reshape(1024, 128).astype(BF), mix[...]).astype(BF)
    for cp in lefts:
        cp.wait_send()
    for q in range(4):
        for half in range(2):
            @pl.when(jnp.logical_not(jnp.logical_and(p == 2 * s + half, q == s)))
            def _(q=q, half=half):
                right_copy(q, half).wait_send()


def local(
    features, conv_weight, conv_bias, species_table, species_id, norm_gain,
    qkv_weight, out_weight, left_weight, right_weight, mix_weight,
):
    any_ = pl.BlockSpec(memory_space=pl.ANY)
    vm = pl.BlockSpec(memory_space=pltpu.VMEM)
    seq_out, left, right = pl.pallas_call(
        main_kernel,
        out_shape=(
            jax.ShapeDtypeStruct((256, D), BF),
            jax.ShapeDtypeStruct((16, 128), BF),
            jax.ShapeDtypeStruct((16, 128), F32),
        ),
        in_specs=[any_] * 4 + [vm] * 6,
        out_specs=(vm, vm, vm),
        scratch_shapes=[
            pltpu.VMEM((ROWS, D), BF),
            pltpu.VMEM((3, 5, 256, D), BF),
            pltpu.VMEM((6, ROWS + 8, 128), F32),
            pltpu.VMEM((3, 48, D), BF),
            pltpu.VMEM((3, 4, 4, 48, D), BF),
            pltpu.VMEM((2, 4, 4, 48, D), BF),
            pltpu.VMEM((2, 3, 1024, 256), BF),
            pltpu.VMEM((3, 256, 256), BF),
            pltpu.VMEM((256, D), BF),
            pltpu.VMEM((1024, D), BF),
            pltpu.VMEM((3, 2, 1024, HEAD), BF),
            pltpu.VMEM((4, 2, 256, HEAD), BF),
            pltpu.VMEM((256, D), BF),
            pltpu.VMEM((4, D), F32),
            pltpu.SemaphoreType.DMA((N_SITES,)),
            pltpu.SemaphoreType.DMA((N_SITES,)),
            pltpu.SemaphoreType.DMA((7,)),
        ],
        compiler_params=pltpu.CompilerParams(
            collective_id=0, has_side_effects=True, vmem_limit_bytes=62 * 2**20
        ),
        name="window",
    )(
        features.reshape(512, D), conv_weight, qkv_weight, out_weight, conv_bias[None], norm_gain[None],
        species_table, species_id, left_weight, right_weight,
    )
    pair_map = pl.pallas_call(
        pair_kernel,
        out_shape=jax.ShapeDtypeStruct((1024, 128), BF),
        in_specs=[vm, vm, vm],
        out_specs=vm,
        scratch_shapes=[
            pltpu.VMEM((8, 16, 128), BF),
            pltpu.VMEM((8, 8, 128), F32),
            pltpu.SemaphoreType.DMA((8,)),
            pltpu.SemaphoreType.DMA((8,)),
            pltpu.SemaphoreType.DMA((8,)),
            pltpu.SemaphoreType.DMA((8,)),
        ],
        compiler_params=pltpu.CompilerParams(collective_id=1, has_side_effects=True),
        name="pairs",
    )(left, right, mix_weight)
    return seq_out[None, None], pair_map.reshape(1, 8, 16, 8, 128)


def solution(mesh):
    return jax.shard_map(
        local,
        mesh=mesh,
        in_specs=(
            P("dp", "pair", "seq", None),
            P(None, "pair", None),
            P(),
            P(),
            P("dp", None),
            P(),
            P(None, ("pair", "dp"), None),
            P(("pair", "dp"), None),
            P(),
            P(),
            P(),
        ),
        out_specs=(P("dp", "pair", "seq", None), P("dp", None, "seq", "pair", None)),
        check_vma=False,
    )
```

```python
import math

import jax
import jax.numpy as jnp
from jax import lax
from jax.experimental import pallas as pl
from jax.experimental.pallas import tpu as pltpu
from jax.sharding import PartitionSpec as P

D = 1536
HEAD = 192
POOL = 16
SPECIES = 2
MESH = pl.DeviceIdType.MESH
BF = jnp.bfloat16
F32 = jnp.float32
HALF = 768
ROWS = 1120


def coords():
    s, p, y = lax.axis_index("seq"), lax.axis_index("pair"), lax.axis_index("dp")
    hi, c = lax.div(s, 2), lax.rem(s, 2)
    z, lo = lax.div(p, 2), lax.rem(p, 2)
    return s, p, y, hi, c, z, lo, 2 * hi + lo


def dev(x, y, z, c):
    return (2 * lax.div(x, 2) + c, 2 * z + lax.rem(x, 2), y)


def m4(v):
    return lax.rem(v + 4, 4)


def nt(a, b):
    return lax.dot_general(a, b, (((1,), (1,)), ((), ())), preferred_element_type=F32)


def nn(a, b):
    return lax.dot_general(a, b, (((1,), (0,)), ((), ())), preferred_element_type=F32)


def al(v, n):
    return pl.multiple_of(v, n)


class Sites:
    def __init__(self, ss, rs):
        self.ss, self.rs, self.n, self.all = ss, rs, 0, []

    def make(self, src, dst, device, pend=True):
        k = self.n
        self.n += 1
        cp = pltpu.make_async_remote_copy(
            src_ref=src, dst_ref=dst, send_sem=self.ss.at[k], recv_sem=self.rs.at[k],
            device_id=device, device_id_type=MESH,
        )
        if pend:
            self.all.append(cp)
        return cp

    def go(self, src, dst, device):
        cp = self.make(src, dst, device)
        cp.start()
        return cp

    def either(self, first, ref_a, ref_b, device):
        a = self.make(ref_a, ref_a, device)
        self.n -= 1
        b = self.make(ref_b, ref_b, device, pend=False)
        pl.when(first)(a.start)
        pl.when(jnp.logical_not(first))(b.start)
        return a


N_SITES = 240
CHUNKS = [
    (0, 0, 2), (0, 2, 4), (0, 4, 5),
    (1, 0, 2), (1, 2, 4), (1, 4, 5),
    (2, 0, 1), (2, 1, 3), (2, 3, 5),
]
ORDER = [
    ("Z", 0), ("Z", 1), ("A", 0), ("Z", 2), ("A", 1), ("Z", 3), ("B", 0), ("Y", 0), ("A", 2), ("Z", 4),
    ("B", 1), ("Y", 1), ("C", 0), ("Y", 2), ("A", 3), ("Z", 5), ("B", 2), ("C", 1), ("A", 4), ("Z", 6),
    ("Y", 3), ("B", 3), ("C", 2), ("A", 5), ("Z", 7), ("B", 4), ("Y", 4), ("A", 6), ("Z", 8), ("C", 3),
    ("B", 5), ("Y", 5), ("F", 0), ("T", 0, 0), ("T", 0, 1), ("A", 7), ("B", 6), ("C", 4), ("C", 5), ("Y", 6),
    ("T", 0, 2), ("T", 0, 3), ("A", 8), ("g0",), ("T", 0, 4), ("B", 7), ("C", 6), ("Y", 7), ("S", 0),
    ("T", 1, 0), ("B", 8), ("Y", 8), ("T", 1, 1), ("T", 1, 2), ("T", 1, 3), ("T", 1, 4), ("g+",), ("g-",),
    ("gP", 0), ("S", 1), ("X", 0), ("W", 0), ("C", 7), ("T", 2, 0), ("C", 8), ("T", 2, 1), ("gP", -1),
    ("T", 2, 2), ("gb",), ("T", 2, 3), ("T", 2, 4), ("gP", 1), ("S", 2), ("X", 1), ("W", 1), ("gP", 2),
    ("o0",), ("X", 2), ("W", 2), ("gQ",), ("N", 0), ("o+",), ("o-",), ("oP", 0), ("N", 1), ("V", 0), ("V", 1),
    ("ob",), ("oP", -1), ("D", 0), ("oP", 1), ("D", 1), ("oQ", 0), ("D", 2), ("oP", 2), ("D", 3), ("oQ", -1),
    ("oQ", 1), ("oQ", 2), ("O", 0), ("O", 1),
]


def by_window(v):
    return jnp.concatenate(
        [v[:, at:at + 64] for a in range(2) for n in range(3) for at in [(2 * b + a) * HEAD + n * 64 for b in range(4)]],
        axis=1,
    )


def main_kernel(
    feat, cw_in, qkv_in, out_in, bias_in, gain_in, table_in, id_in, lw, rw, mix,
    seq_out, pair_out,
    F, CW, acc, QT, AW, OW, TH, TA, TOK, NM, QH, AO, AT, BO, MX, VEC, LW, RW, L, R,
    ss, rs, ls, ssr, rsr,
):
    s, p, y, hi, c, z, lo, x = coords()
    xp, xm, x2 = m4(x + 1), m4(x - 1), m4(x + 2)
    sib = dev(x, y, z, 1 - c)
    st = Sites(ss, rs)

    barrier = pltpu.get_barrier_semaphore()
    peers = [sib]
    for xx in (xp, xm, x2):
        peers += [dev(xx, y, z, c), dev(xx, y, z, 1 - c)]
    for d in (1, -1):
        peers += [dev(x, m4(y + d), z, c), dev(x, y, m4(z + d), c)]
    peers += [(s, lax.rem(p + d, 8), y) for d in range(1, 8)]
    for t in peers:
        pl.semaphore_signal(barrier, inc=1, device_id=t, device_id_type=MESH)
    inside = lax.div(p, 2) == s
    for w in range(8):
        @pl.when(jnp.logical_not(jnp.logical_and(inside, p == w)))
        def _(w=w):
            pl.semaphore_signal(barrier, inc=1, device_id=(lax.div(p, 2), w, y), device_id_type=MESH)

    lcopies = []

    def local(src, dst):
        cp = pltpu.make_async_copy(src, dst, ls.at[len(lcopies)])
        cp.start()
        lcopies.append(cp)
        return cp

    cols = pl.ds(al(c * HALF, 128), HALF)
    own_q = local(qkv_in, QT)
    own_f = local(feat, F.at[pl.ds(16, 512)])
    own_o = local(out_in.at[:, cols], OW.at[lo, z, y, :, cols])
    own_w = [local(cw_in.at[:, pl.ds(64 * n, 64)], CW.at[n, :, pl.ds(al(z * 64, 16), 64)]) for n in range(3)]

    VEC[0:1] = by_window(bias_in[...].reshape(1, D))
    VEC[1:2] = by_window(gain_in[...].reshape(1, D))
    VEC[2:4] = by_window(table_in[...])
    own_q.wait()
    for k in range(3):
        QT[k] = by_window(QT[k])
    pl.semaphore_wait(barrier, len(peers) + 8 - inside.astype(jnp.int32))

    def turn(k):
        g = lax.rem(y + c, 2)
        sgn = 1 - 2 * g
        return g, m4(z + sgn), m4(z - sgn), m4(z + 2)

    def to_z(k):
        return dev(x, y, turn(k)[1], c)

    def part(k, slot, off, rows):
        n, t0, t1 = CHUNKS[k]
        return CW.at[n, pl.ds(t0, t1 - t0), pl.ds(al(slot * 64 + c * 32 + off, 16), rows)]

    zA, zB, yA, yC, sb = {}, {}, {}, {}, {}

    def same(ref, device):
        return st.go(ref, ref, device)

    def start_zA(k):
        n, t0, t1 = CHUNKS[k]
        src = cw_in.at[pl.ds(t0, t1 - t0), pl.ds(al(n * 64 + c * 32, 16), 32)]
        zA[k] = st.go(src, part(k, z, 0, 32), to_z(k))

    def pass_zA(k):
        zA[k].wait_recv()
        g, zd, zs, zo = turn(k)
        zB[k] = same(part(k, zs, 16 * g, 16), to_z(k))
        yA[k] = [
            same(part(k, zs, 0, 16), dev(x, m4(y + 1), z, c)),
            same(part(k, zs, 16, 16), dev(x, m4(y - 1), z, c)),
        ]
        sb[k] = [same(part(k, zs, 0, 32), sib)]

    def pass_zB(k):
        zB[k].wait_recv()
        g, zd, zs, zo = turn(k)
        yC[k] = same(part(k, zo, 16 * g, 16), dev(x, m4(y + 1 - 2 * c), z, c))

    def pass_yA(k):
        for cp in yA[k]:
            cp.wait_recv()
        sb[k].append(same(part(k, turn(k)[1], 0, 32), sib))

    def pass_yC(k):
        yC[k].wait_recv()
        sb[k].append(same(part(k, m4(z + 2), 0, 32), sib))

    start_zA(0)

    mine_q = AW.at[:, z, y, :, cols]
    inner = jnp.logical_or(x == 1, x == 2).astype(jnp.int32)
    third = pl.ds(al(c * HALF + 384 * (1 - inner), 128), 384)
    swap_q = [pltpu.make_async_remote_copy(
        src_ref=QT.at[:, :, third], dst_ref=AW.at[:, z, y, :, third], send_sem=ss.at[N_SITES],
        recv_sem=rs.at[N_SITES + at], device_id=dev(3 - lo, y, z, c), device_id_type=MESH,
    ) for at in (1 - inner, 0, 1)]
    swap_q[0].start()
    keep_q = pltpu.make_async_copy(QT.at[:, :, cols], mine_q, ls.at[6])

    @pl.when(hi == 0)
    def _():
        keep_q.start()

    swap_o = []
    for k, xx in enumerate((xp, xm)):
        sub = pl.ds(al(c * HALF + 384 * k, 128), 384)
        swap_o.append(st.go(out_in.at[:, sub], OW.at[lo, z, y, :, sub], dev(xx, y, z, c)))

    lastr, firstr = feat.at[pl.ds(496, 16)], feat.at[pl.ds(0, 16)]
    xn = m4(x + 2 * c)
    xq = m4(x + 2 * (1 - c))
    halo = [
        st.go(lastr, F.at[pl.ds(0, 16)], dev(xn, y, z, 1 - c)),
        st.go(firstr, F.at[pl.ds(528, 16)], dev(xq, y, z, 1 - c)),
        st.go(lastr, F.at[pl.ds(544, 16)], dev(m4(xn + 1), y, z, 1 - c)),
        st.go(firstr, F.at[pl.ds(1104, 16)], dev(m4(xq - 1), y, z, 1 - c)),
        st.go(feat.at[pl.ds(0, 272)], F.at[pl.ds(560, 272)], dev(xp, y, z, c)),
        st.go(feat.at[pl.ds(240, 272)], F.at[pl.ds(832, 272)], dev(xm, y, z, c)),
    ]

    acc[...] = jnp.zeros_like(acc)

    def ready_features():
        own_f.wait()
        own_o.wait()
        for cp in own_w:
            cp.wait()
        for cp in halo:
            cp.wait_recv()
        sa = 2 * lax.div(xm, 2) + c
        sbk = 2 * lax.div(xp, 2) + c
        for cond, at in ((s == 0, 0), (s == 3, 528), (sa == 0, 544), (sbk == 3, 1104)):
            @pl.when(cond)
            def _(at=at):
                F[at:at + 16] = jnp.zeros((16, D), BF)

    def wait_swap():
        @pl.when(hi == 0)
        def _():
            keep_q.wait()

        @pl.when(hi == 1)
        def _():
            swap_q[1].wait_recv()
            swap_q[2].wait_recv()

    def conv_tap(n, t):
        for k, (m, t0, t1) in enumerate(CHUNKS):
            if m == n and t0 <= t < t1 and sb[k]:
                for cp in sb[k]:
                    cp.wait_recv()
                sb[k] = []
        out = nt(F[...], CW[n, t])
        for j in range(2):
            acc[2 * n + j, 4 - t:4 - t + ROWS] += out[:, 128 * j:128 * j + 128]

    i0, k0 = (1 - c) * y + c * z, (1 - c) * z + c * y

    class Gather:
        def __init__(self, buf):
            self.buf = buf
            self.b1, self.a2, self.b2 = [], {}, {}

        def ref(self, i, k, sub=None):
            zz, yy = (1 - c) * k + c * i, (1 - c) * i + c * k
            if sub is None:
                return self.buf.at[:, zz, yy, :, cols]
            return self.buf.at[:, zz, yy, :, pl.ds(al(c * HALF + 384 * sub, 128), 384)]

        def to(self, i, k):
            return dev(x, (1 - c) * i + c * k, (1 - c) * k + c * i, c)

        def second(self, j):
            i = m4(i0 + j)
            own = self.ref(i, k0)
            self.a2[j] = [same(own, self.to(i0, m4(k0 + d))) for d in (1, -1)]

        def second_pass(self, j):
            i = m4(i0 + j)
            self.a2[j][0].wait_recv()
            self.b2[j] = [same(self.ref(i, m4(k0 - 1), 0), self.to(i0, m4(k0 + 1)))]
            self.a2[j][1].wait_recv()
            self.b2[j].append(same(self.ref(i, m4(k0 + 1), 1), self.to(i0, m4(k0 - 1))))

        def p0(self):
            own = self.ref(i0, k0)
            self.a1 = [same(own, self.to(m4(i0 + d), k0)) for d in (1, -1)]
            self.second(0)

        def p1(self, sign):
            if sign > 0:
                self.a1[0].wait_recv()
                self.b1.append(same(self.ref(m4(i0 - 1), k0, 0), self.to(m4(i0 + 1), k0)))
                self.second(-1)
            else:
                self.a1[1].wait_recv()
                self.b1.append(same(self.ref(m4(i0 + 1), k0, 1), self.to(m4(i0 - 1), k0)))
                self.second(1)

        def p2(self):
            for cp in self.b1:
                cp.wait_recv()
            self.second(2)

        def p5(self, js):
            for j in js:
                for cp in self.b2[j]:
                    cp.wait_recv()

        def to_sib(self, js):
            self.p5(js)
            for j in js:
                i = m4(i0 + j)
                a, b = self.buf.at[:, :, i, :, cols], self.buf.at[:, i, :, :, cols]
                to_core.append(st.either(c == 0, a, b, sib))

    gq, go = Gather(AW), Gather(OW)
    to_core = []

    s2 = 2 * (1 - hi) + c
    blk = pl.ds(al(s * 256, 256), 256)
    blk2 = pl.ds(al(s2 * 256, 256), 256)
    a0 = (2 * lax.div(xm, 2) + c) * 256
    b0 = (2 * lax.div(xp, 2) + c) * 256 + 128
    ids = id_in[...]
    lane = lax.broadcasted_iota(jnp.int32, (1, 8), 1)

    def piece(row, n):
        both = [VEC[row:row + 1, a * HALF + n * 256:a * HALF + n * 256 + 256] for a in range(2)]
        return jnp.where(jnp.full((1, 256), lo, jnp.int32) == 0, both[0], both[1])

    def tokens(at, window, n):
        kind = jnp.sum(jnp.where(lane == window, ids, 0), axis=1, keepdims=True)
        species = jnp.where(jnp.broadcast_to(kind, (1, 256)) == 0, piece(2, n), piece(3, n))
        bias = piece(0, n)
        cut = []
        for j in range(2):
            lanes = slice(128 * j, 128 * j + 128)
            even = jax.nn.gelu(acc[2 * n + j, pl.ds(at, 128, stride=2), :] + bias[:, lanes])
            odd = jax.nn.gelu(acc[2 * n + j, pl.ds(at + 1, 128, stride=2), :] + bias[:, lanes])
            cut.append((jnp.maximum(even, odd) + species[:, lanes]).astype(BF))
        return jnp.concatenate(cut, axis=1)

    cross, far, near = {}, {}, {}

    def send_tokens(n):
        wo = 2 * z + (1 - lo)
        TA[n, 0:128] = tokens(562, wo, n)
        TA[n, 128:256] = tokens(850, wo, n)
        ta, tb = TH.at[lo, n, pl.ds(al(a0, 128), 128)], TH.at[lo, n, pl.ds(al(b0, 128), 128)]
        cross[n] = []
        for xx in (xp, xm):
            cross[n] += [
                st.go(TA.at[n, pl.ds(0, 128)], ta, dev(xx, y, z, c)),
                st.go(TA.at[n, pl.ds(128, 128)], tb, dev(xx, y, z, c)),
            ]
        TH[lo, n, pl.ds(al(s * 256, 256), 128)] = tokens(18, p, n)
        TH[lo, n, pl.ds(al(s * 256 + 128, 128), 128)] = tokens(274, p, n)
        far[n] = same(TH.at[lo, n, blk], dev(x2, y, z, c))
        near[n] = [same(TH.at[lo, n, blk], sib)]

    def pass_cross(n):
        for cp in cross[n]:
            cp.wait_recv()
        near[n].append(same(TH.at[1 - lo, n, blk], sib))
        near[n].append(same(TH.at[1 - lo, n, blk2], sib))

    def pass_far(n):
        far[n].wait_recv()
        near[n].append(same(TH.at[lo, n, blk2], sib))

    def norm(block):
        at = pl.ds(al(block * 256, 256), 256)
        ms = 0.0
        for a in range(2):
            for n in range(3):
                h = TH[a, n, at].astype(F32)
                ms = ms + jnp.sum(h * h, axis=1, keepdims=True)
        r = lax.rsqrt(ms / D + 1e-05)
        for a in range(2):
            for n in range(3):
                lanes = slice(a * HALF + n * 256, a * HALF + n * 256 + 256)
                NM[at, lanes] = (TH[a, n, at].astype(F32) * r * VEC[1:2, lanes]).astype(BF)

    def start_gq():
        wait_swap()
        gq.p0()

    def start_go():
        for cp in swap_o:
            cp.wait_recv()
        go.p0()

    sq = []

    def finish_gq():
        gq.p5((0, -1, 1, 2))
        other = pl.ds(al(2 * (1 - c), 2), 2)
        sq.append(same(AW.at[:, other, :, :, cols], sib))

    def norms(k):
        if k == 0:
            norm(s)
            norm(s2)
            hs = {(a, n): TH[a, n, blk] for a in range(2) for n in range(3)}
            TOK[...] = jnp.concatenate(
                [hs[a, n][:, b * 64:(b + 1) * 64] for b in range(4) for a in range(2) for n in range(3)], axis=1
            )
        else:
            for n in range(3):
                for cp in near[n]:
                    cp.wait_recv()
            norm(2 * hi + 1 - c)
            norm(2 * (1 - hi) + 1 - c)

    heads = pl.ds(al(2 * c, 2), 2)

    def keys_values(k):
        if k == 0:
            sq[0].wait_recv()
        w = AW[1:3, heads].reshape(4 * HEAD, D)
        for b in (s, s2) if k == 0 else (2 * hi + 1 - c, 2 * (1 - hi) + 1 - c):
            at = pl.ds(al(b * 256, 256), 256)
            res = nt(NM[at], w).astype(BF)
            for h in range(4):
                QH[1 + h // 2, h % 2, at] = res[:, h * HEAD:(h + 1) * HEAD]

    scale = math.log2(math.e) / math.sqrt(HEAD)
    lop = lax.rem(lo + hi, 2)
    my_cols = pl.ds(al(c * 384, 128), 384)
    back = []
    dests = [(1 - hi, c, x2, c), (1 - hi, 1 - c, x2, 1 - c), (hi, 1 - c, x, 1 - c), (hi, c, None, None)]

    def attend(d):
        dhi, dc, dx, dcc = dests[d]
        at = pl.ds(al((2 * dhi + dc) * 256, 256), 256)
        res = nt(NM[at], AW[0, heads].reshape(2 * HEAD, D)).astype(BF)
        for h in range(2):
            QH[0, h, at] = res[:, h * HEAD:(h + 1) * HEAD]
        for h in range(2):
            sc = nt(QH[0, h, at], QH[1, h])
            e = jnp.exp2((sc - jnp.max(sc, axis=1, keepdims=True)) * scale)
            inv = 1.0 / jnp.sum(e, axis=1, keepdims=True)
            AO[d, h] = (nn(e.astype(BF), QH[2, h]) * inv).astype(BF)
        both = jnp.concatenate([AO[d, 0], AO[d, 1]], axis=1)
        if dx is None:
            AT[lop, :, my_cols] = both
        else:
            BO[d] = both
            back.append(st.go(BO.at[d], AT.at[lop, :, my_cols], dev(dx, y, z, dcc)))

    def project(k):
        if k == 0:
            for cp in to_core:
                cp.wait_recv()
            back[2].wait_recv()

            def body(n, carry):
                at = pl.ds(al(n * 256, 256), 256)
                MX[:, at] = TOK[:, at].astype(F32) + nn(AT[lop], OW[lop, :, :, :, at].reshape(HALF, 256))
                return carry
        else:
            for cp in back[:2]:
                cp.wait_recv()

            def body(n, carry):
                at = pl.ds(al(n * 256, 256), 256)
                mixed = nn(AT[1 - lop], OW[1 - lop, :, :, :, at].reshape(HALF, 256))
                seq_out[:, at] = (MX[:, at] + mixed).astype(BF)
                return carry
        lax.fori_loop(0, 6, body, 0)

    done = {
        "Z": lambda k: k == 0 or start_zA(k), "A": pass_zA, "B": pass_zB, "Y": pass_yA, "C": pass_yC,
        "F": lambda k: ready_features(), "T": conv_tap, "S": send_tokens, "X": pass_cross, "W": pass_far,
        "g0": start_gq, "g+": lambda: gq.p1(1), "g-": lambda: gq.p1(-1), "gb": gq.p2, "gP": gq.second_pass,
        "gQ": finish_gq,
        "o0": start_go, "o+": lambda: go.p1(1), "o-": lambda: go.p1(-1), "ob": go.p2, "oP": go.second_pass,
        "oQ": lambda j: go.to_sib((j,)),
        "N": norms, "V": keys_values, "D": attend, "O": project,
    }
    for what, *at in ORDER:
        if what == "O" and at[0] == 1:
            sent = len(st.all) - 3
            for cp in st.all[:sent]:
                cp.wait_send()
        done[what](*at)

    rows = jnp.sum(seq_out[...].astype(F32).reshape(16, POOL, D), axis=1) * (1.0 / POOL)
    unit = (rows * lax.rsqrt(jnp.mean(rows * rows, axis=1, keepdims=True) + 1e-05)).astype(BF)
    LW[...] = nn(unit, lw[...]).astype(BF)
    RW[...] = nn(unit, rw[...]).astype(BF).astype(F32)

    lefts = [st.go(LW, L.at[p], (s, lax.rem(p + d, 8), y)) for d in range(1, 8)]
    L[p] = LW[...]

    def right_copy(q, half):
        return pltpu.make_async_remote_copy(
            src_ref=RW.at[pl.ds(8 * half, 8)], dst_ref=R.at[p], send_sem=ssr.at[2 * q + half],
            recv_sem=rsr.at[p], device_id=(q, 2 * s + half, y), device_id_type=MESH,
        )

    for q in range(4):
        for half in range(2):
            me = jnp.logical_and(p == 2 * s + half, q == s)

            @pl.when(jnp.logical_not(me))
            def _(q=q, half=half):
                right_copy(q, half).start()

            @pl.when(me)
            def _(half=half):
                R[p] = RW[8 * half:8 * half + 8, :]

    for cp in lefts:
        cp.wait_recv()
    for w in range(8):
        @pl.when(jnp.logical_not(jnp.logical_and(inside, p == w)))
        def _(w=w):
            pltpu.make_async_remote_copy(
                src_ref=RW.at[pl.ds(0, 8)], dst_ref=R.at[w], send_sem=ssr.at[0],
                recv_sem=rsr.at[w], device_id=(s, p, y), device_id_type=MESH,
            ).wait_recv()

    outer = L[...].astype(F32)[:, :, None, :] * R[...][:, None, :, :]
    pair_out[...] = nn(outer.reshape(1024, 128).astype(BF), mix[...]).astype(BF)

    for cp in st.all[sent:]:
        cp.wait_send()
    swap_q[0].wait_send()
    for q in range(4):
        for half in range(2):
            @pl.when(jnp.logical_not(jnp.logical_and(p == 2 * s + half, q == s)))
            def _(q=q, half=half):
                right_copy(q, half).wait_send()


def local(
    features, conv_weight, conv_bias, species_table, species_id, norm_gain,
    qkv_weight, out_weight, left_weight, right_weight, mix_weight,
):
    any_ = pl.BlockSpec(memory_space=pl.ANY)
    vm = pl.BlockSpec(memory_space=pltpu.VMEM)
    seq_out, pair_map = pl.pallas_call(
        main_kernel,
        out_shape=(jax.ShapeDtypeStruct((256, D), BF), jax.ShapeDtypeStruct((1024, 128), BF)),
        in_specs=[any_] * 4 + [vm] * 7,
        out_specs=(vm, vm),
        scratch_shapes=[
            pltpu.VMEM((ROWS, D), BF),
            pltpu.VMEM((3, 5, 256, D), BF),
            pltpu.VMEM((6, ROWS + 8, 128), F32),
            pltpu.VMEM((3, 48, D), BF),
            pltpu.VMEM((3, 4, 4, 48, D), BF),
            pltpu.VMEM((2, 4, 4, 48, D), BF),
            pltpu.VMEM((2, 3, 1024, 256), BF),
            pltpu.VMEM((3, 256, 256), BF),
            pltpu.VMEM((256, D), BF),
            pltpu.VMEM((1024, D), BF),
            pltpu.VMEM((3, 2, 1024, HEAD), BF),
            pltpu.VMEM((4, 2, 256, HEAD), BF),
            pltpu.VMEM((2, 256, HALF), BF),
            pltpu.VMEM((3, 256, 384), BF),
            pltpu.VMEM((256, D), F32),
            pltpu.VMEM((4, D), F32),
            pltpu.VMEM((16, 128), BF),
            pltpu.VMEM((16, 128), F32),
            pltpu.VMEM((8, 16, 128), BF),
            pltpu.VMEM((8, 8, 128), F32),
            pltpu.SemaphoreType.DMA((N_SITES + 2,)),
            pltpu.SemaphoreType.DMA((N_SITES + 2,)),
            pltpu.SemaphoreType.DMA((7,)),
            pltpu.SemaphoreType.DMA((8,)),
            pltpu.SemaphoreType.DMA((8,)),
        ],
        compiler_params=pltpu.CompilerParams(
            collective_id=0, has_side_effects=True, vmem_limit_bytes=62 * 2**20
        ),
        name="window",
    )(
        features.reshape(512, D), conv_weight, qkv_weight, out_weight, conv_bias, norm_gain,
        species_table, species_id, left_weight, right_weight, mix_weight,
    )
    return seq_out[None, None], pair_map.reshape(1, 8, 16, 8, 128)


def solution(mesh):
    return jax.shard_map(
        local,
        mesh=mesh,
        in_specs=(
            P("dp", "pair", "seq", None),
            P(None, "pair", None),
            P(),
            P(),
            P("dp", None),
            P(),
            P(None, ("pair", "dp"), None),
            P(("pair", "dp"), None),
            P(),
            P(),
            P(),
        ),
        out_specs=(P("dp", "pair", "seq", None), P("dp", None, "seq", "pair", None)),
        check_vma=False,
    )
```

```python
import math

import jax
import jax.numpy as jnp
from jax import lax
from jax.experimental import pallas as pl
from jax.experimental.pallas import tpu as pltpu
from jax.sharding import PartitionSpec as P

D = 1536
HEAD = 192
POOL = 16
SPECIES = 2
MESH = pl.DeviceIdType.MESH
BF = jnp.bfloat16
F32 = jnp.float32
HALF = 768
ROWS = 1120


def coords():
    s, p, y = lax.axis_index("seq"), lax.axis_index("pair"), lax.axis_index("dp")
    hi, c = lax.div(s, 2), lax.rem(s, 2)
    z, lo = lax.div(p, 2), lax.rem(p, 2)
    return s, p, y, hi, c, z, lo, 2 * hi + lo


def dev(x, y, z, c):
    return (2 * lax.div(x, 2) + c, 2 * z + lax.rem(x, 2), y)


def m4(v):
    return lax.rem(v + 4, 4)


def nt(a, b):
    return lax.dot_general(a, b, (((1,), (1,)), ((), ())), preferred_element_type=F32)


def nn(a, b):
    return lax.dot_general(a, b, (((1,), (0,)), ((), ())), preferred_element_type=F32)


def al(v, n):
    return pl.multiple_of(v, n)


class Sites:
    def __init__(self, ss, rs):
        self.ss, self.rs, self.n, self.all = ss, rs, 0, []

    def make(self, src, dst, device, pend=True):
        k = self.n
        self.n += 1
        cp = pltpu.make_async_remote_copy(
            src_ref=src, dst_ref=dst, send_sem=self.ss.at[k], recv_sem=self.rs.at[k],
            device_id=device, device_id_type=MESH,
        )
        if pend:
            self.all.append(cp)
        return cp

    def go(self, src, dst, device):
        cp = self.make(src, dst, device)
        cp.start()
        return cp

    def either(self, first, ref_a, ref_b, device):
        a = self.make(ref_a, ref_a, device)
        self.n -= 1
        b = self.make(ref_b, ref_b, device, pend=False)
        pl.when(first)(a.start)
        pl.when(jnp.logical_not(first))(b.start)
        return a


N_SITES = 240
CHUNKS = [
    (0, 0, 2), (0, 2, 4), (0, 4, 5),
    (1, 0, 2), (1, 2, 4), (1, 4, 5),
    (2, 0, 1), (2, 1, 3), (2, 3, 5),
]
ORDER = [
    ("Z", 0), ("Z", 1), ("A", 0), ("Z", 2), ("A", 1), ("Z", 3), ("B", 0), ("Y", 0), ("A", 2), ("Z", 4),
    ("B", 1), ("Y", 1), ("C", 0), ("Y", 2), ("A", 3), ("Z", 5), ("B", 2), ("C", 1), ("A", 4), ("Z", 6),
    ("Y", 3), ("B", 3), ("C", 2), ("A", 5), ("Z", 7), ("B", 4), ("Y", 4), ("A", 6), ("Z", 8), ("C", 3),
    ("B", 5), ("Y", 5), ("F", 0), ("T", 0, 0), ("T", 0, 1), ("A", 7), ("B", 6), ("C", 4), ("C", 5), ("Y", 6),
    ("T", 0, 2), ("T", 0, 3), ("A", 8), ("g0",), ("T", 0, 4), ("B", 7), ("C", 6), ("Y", 7), ("S", 0),
    ("T", 1, 0), ("B", 8), ("Y", 8), ("T", 1, 1), ("T", 1, 2), ("T", 1, 3), ("T", 1, 4), ("g+",), ("g-",),
    ("gP", 0), ("S", 1), ("X", 0), ("W", 0), ("C", 7), ("T", 2, 0), ("C", 8), ("T", 2, 1), ("gP", -1),
    ("T", 2, 2), ("gb",), ("o0",), ("T", 2, 3), ("T", 2, 4), ("gP", 1), ("S", 2), ("X", 1), ("W", 1),
    ("gP", 2), ("o+",), ("o-",), ("X", 2), ("oP", 0), ("ob",), ("W", 2), ("gQ",), ("N", 0), ("N", 1),
    ("V", 0), ("V", 1), ("D", 0), ("D", 1), ("oP", -1), ("oP", 1), ("oQ", 0), ("D", 2), ("oP", 2), ("D", 3),
    ("oQ", -1), ("oQ", 1), ("oQ", 2), ("O", 0), ("O", 1),
]


def by_window(v):
    return jnp.concatenate(
        [v[:, at:at + 64] for a in range(2) for n in range(3) for at in [(2 * b + a) * HEAD + n * 64 for b in range(4)]],
        axis=1,
    )


def main_kernel(
    feat, cw_in, qkv_in, out_in, bias_in, gain_in, table_in, id_in, lw, rw, mix,
    seq_out, pair_out,
    F, CW, acc, QT, AW, OW, TH, TA, TOK, NM, QH, AO, AT, BO, MX, VEC, LW, RW, L, R,
    ss, rs, ls, ssr, rsr,
):
    s, p, y, hi, c, z, lo, x = coords()
    xp, xm, x2 = m4(x + 1), m4(x - 1), m4(x + 2)
    sib = dev(x, y, z, 1 - c)
    st = Sites(ss, rs)

    barrier = pltpu.get_barrier_semaphore()
    peers = [sib]
    for xx in (xp, xm, x2):
        peers += [dev(xx, y, z, c), dev(xx, y, z, 1 - c)]
    for d in (1, -1):
        peers += [dev(x, m4(y + d), z, c), dev(x, y, m4(z + d), c)]
    peers += [(s, lax.rem(p + d, 8), y) for d in range(1, 8)]
    for t in peers:
        pl.semaphore_signal(barrier, inc=1, device_id=t, device_id_type=MESH)
    inside = lax.div(p, 2) == s
    for w in range(8):
        @pl.when(jnp.logical_not(jnp.logical_and(inside, p == w)))
        def _(w=w):
            pl.semaphore_signal(barrier, inc=1, device_id=(lax.div(p, 2), w, y), device_id_type=MESH)

    lcopies = []

    def local(src, dst):
        cp = pltpu.make_async_copy(src, dst, ls.at[len(lcopies)])
        cp.start()
        lcopies.append(cp)
        return cp

    cols = pl.ds(al(c * HALF, 128), HALF)
    own_q = local(qkv_in, QT)
    own_f = local(feat, F.at[pl.ds(16, 512)])
    own_o = local(out_in.at[:, cols], OW.at[lo, z, y, :, cols])
    own_w = [local(cw_in.at[:, pl.ds(64 * n, 64)], CW.at[n, :, pl.ds(al(z * 64, 16), 64)]) for n in range(3)]

    VEC[0:1] = by_window(bias_in[...].reshape(1, D))
    VEC[1:2] = by_window(gain_in[...].reshape(1, D))
    VEC[2:4] = by_window(table_in[...])
    own_q.wait()
    for k in range(3):
        QT[k] = by_window(QT[k])
    pl.semaphore_wait(barrier, len(peers) + 8 - inside.astype(jnp.int32))

    def turn(k):
        g = lax.rem(y + c, 2)
        sgn = 1 - 2 * g
        return g, m4(z + sgn), m4(z - sgn), m4(z + 2)

    def to_z(k):
        return dev(x, y, turn(k)[1], c)

    def part(k, slot, off, rows):
        n, t0, t1 = CHUNKS[k]
        return CW.at[n, pl.ds(t0, t1 - t0), pl.ds(al(slot * 64 + c * 32 + off, 16), rows)]

    zA, zB, yA, yC, sb = {}, {}, {}, {}, {}

    def same(ref, device):
        return st.go(ref, ref, device)

    def start_zA(k):
        n, t0, t1 = CHUNKS[k]
        src = cw_in.at[pl.ds(t0, t1 - t0), pl.ds(al(n * 64 + c * 32, 16), 32)]
        zA[k] = st.go(src, part(k, z, 0, 32), to_z(k))

    def pass_zA(k):
        zA[k].wait_recv()
        g, zd, zs, zo = turn(k)
        zB[k] = same(part(k, zs, 16 * g, 16), to_z(k))
        yA[k] = [
            same(part(k, zs, 0, 16), dev(x, m4(y + 1), z, c)),
            same(part(k, zs, 16, 16), dev(x, m4(y - 1), z, c)),
        ]
        sb[k] = [same(part(k, zs, 0, 32), sib)]

    def pass_zB(k):
        zB[k].wait_recv()
        g, zd, zs, zo = turn(k)
        yC[k] = same(part(k, zo, 16 * g, 16), dev(x, m4(y + 1 - 2 * c), z, c))

    def pass_yA(k):
        for cp in yA[k]:
            cp.wait_recv()
        sb[k].append(same(part(k, turn(k)[1], 0, 32), sib))

    def pass_yC(k):
        yC[k].wait_recv()
        sb[k].append(same(part(k, m4(z + 2), 0, 32), sib))

    start_zA(0)

    mine_q = AW.at[:, z, y, :, cols]
    inner = jnp.logical_or(x == 1, x == 2).astype(jnp.int32)
    third = pl.ds(al(c * HALF + 384 * (1 - inner), 128), 384)
    swap_q = [pltpu.make_async_remote_copy(
        src_ref=QT.at[:, :, third], dst_ref=AW.at[:, z, y, :, third], send_sem=ss.at[N_SITES],
        recv_sem=rs.at[N_SITES + at], device_id=dev(3 - lo, y, z, c), device_id_type=MESH,
    ) for at in (1 - inner, 0, 1)]
    swap_q[0].start()
    keep_q = pltpu.make_async_copy(QT.at[:, :, cols], mine_q, ls.at[6])

    @pl.when(hi == 0)
    def _():
        keep_q.start()

    swap_o = []
    for k, xx in enumerate((xp, xm)):
        sub = pl.ds(al(c * HALF + 384 * k, 128), 384)
        swap_o.append(st.go(out_in.at[:, sub], OW.at[lo, z, y, :, sub], dev(xx, y, z, c)))

    lastr, firstr = feat.at[pl.ds(496, 16)], feat.at[pl.ds(0, 16)]
    xn = m4(x + 2 * c)
    xq = m4(x + 2 * (1 - c))
    halo = [
        st.go(lastr, F.at[pl.ds(0, 16)], dev(xn, y, z, 1 - c)),
        st.go(firstr, F.at[pl.ds(528, 16)], dev(xq, y, z, 1 - c)),
        st.go(lastr, F.at[pl.ds(544, 16)], dev(m4(xn + 1), y, z, 1 - c)),
        st.go(firstr, F.at[pl.ds(1104, 16)], dev(m4(xq - 1), y, z, 1 - c)),
        st.go(feat.at[pl.ds(0, 272)], F.at[pl.ds(560, 272)], dev(xp, y, z, c)),
        st.go(feat.at[pl.ds(240, 272)], F.at[pl.ds(832, 272)], dev(xm, y, z, c)),
    ]

    acc[...] = jnp.zeros_like(acc)

    def ready_features():
        own_f.wait()
        own_o.wait()
        for cp in own_w:
            cp.wait()
        for cp in halo:
            cp.wait_recv()
        sa = 2 * lax.div(xm, 2) + c
        sbk = 2 * lax.div(xp, 2) + c
        for cond, at in ((s == 0, 0), (s == 3, 528), (sa == 0, 544), (sbk == 3, 1104)):
            @pl.when(cond)
            def _(at=at):
                F[at:at + 16] = jnp.zeros((16, D), BF)

    def wait_swap():
        @pl.when(hi == 0)
        def _():
            keep_q.wait()

        @pl.when(hi == 1)
        def _():
            swap_q[1].wait_recv()
            swap_q[2].wait_recv()

    def conv_tap(n, t):
        for k, (m, t0, t1) in enumerate(CHUNKS):
            if m == n and t0 <= t < t1 and sb[k]:
                for cp in sb[k]:
                    cp.wait_recv()
                sb[k] = []
        out = nt(F[...], CW[n, t])
        for j in range(2):
            acc[2 * n + j, 4 - t:4 - t + ROWS] += out[:, 128 * j:128 * j + 128]

    i0, k0 = (1 - c) * y + c * z, (1 - c) * z + c * y

    class Gather:
        def __init__(self, buf):
            self.buf = buf
            self.b1, self.a2, self.b2 = [], {}, {}

        def ref(self, i, k, sub=None):
            zz, yy = (1 - c) * k + c * i, (1 - c) * i + c * k
            if sub is None:
                return self.buf.at[:, zz, yy, :, cols]
            return self.buf.at[:, zz, yy, :, pl.ds(al(c * HALF + 384 * sub, 128), 384)]

        def to(self, i, k):
            return dev(x, (1 - c) * i + c * k, (1 - c) * k + c * i, c)

        def second(self, j):
            i = m4(i0 + j)
            own = self.ref(i, k0)
            self.a2[j] = [same(own, self.to(i0, m4(k0 + d))) for d in (1, -1)]

        def second_pass(self, j):
            i = m4(i0 + j)
            self.a2[j][0].wait_recv()
            self.b2[j] = [same(self.ref(i, m4(k0 - 1), 0), self.to(i0, m4(k0 + 1)))]
            self.a2[j][1].wait_recv()
            self.b2[j].append(same(self.ref(i, m4(k0 + 1), 1), self.to(i0, m4(k0 - 1))))

        def p0(self):
            own = self.ref(i0, k0)
            self.a1 = [same(own, self.to(m4(i0 + d), k0)) for d in (1, -1)]
            self.second(0)

        def p1(self, sign):
            if sign > 0:
                self.a1[0].wait_recv()
                self.b1.append(same(self.ref(m4(i0 - 1), k0, 0), self.to(m4(i0 + 1), k0)))
                self.second(-1)
            else:
                self.a1[1].wait_recv()
                self.b1.append(same(self.ref(m4(i0 + 1), k0, 1), self.to(m4(i0 - 1), k0)))
                self.second(1)

        def p2(self):
            for cp in self.b1:
                cp.wait_recv()
            self.second(2)

        def p5(self, js):
            for j in js:
                for cp in self.b2[j]:
                    cp.wait_recv()

        def to_sib(self, js):
            self.p5(js)
            for j in js:
                i = m4(i0 + j)
                a, b = self.buf.at[:, :, i, :, cols], self.buf.at[:, i, :, :, cols]
                to_core.append(st.either(c == 0, a, b, sib))

    gq, go = Gather(AW), Gather(OW)
    to_core = []

    s2 = 2 * (1 - hi) + c
    blk = pl.ds(al(s * 256, 256), 256)
    blk2 = pl.ds(al(s2 * 256, 256), 256)
    a0 = (2 * lax.div(xm, 2) + c) * 256
    b0 = (2 * lax.div(xp, 2) + c) * 256 + 128
    ids = id_in[...]
    lane = lax.broadcasted_iota(jnp.int32, (1, 8), 1)

    def piece(row, n):
        both = [VEC[row:row + 1, a * HALF + n * 256:a * HALF + n * 256 + 256] for a in range(2)]
        return jnp.where(jnp.full((1, 256), lo, jnp.int32) == 0, both[0], both[1])

    def tokens(at, window, n):
        kind = jnp.sum(jnp.where(lane == window, ids, 0), axis=1, keepdims=True)
        species = jnp.where(jnp.broadcast_to(kind, (1, 256)) == 0, piece(2, n), piece(3, n))
        bias = piece(0, n)
        cut = []
        for j in range(2):
            lanes = slice(128 * j, 128 * j + 128)
            even = jax.nn.gelu(acc[2 * n + j, pl.ds(at, 128, stride=2), :] + bias[:, lanes])
            odd = jax.nn.gelu(acc[2 * n + j, pl.ds(at + 1, 128, stride=2), :] + bias[:, lanes])
            cut.append((jnp.maximum(even, odd) + species[:, lanes]).astype(BF))
        return jnp.concatenate(cut, axis=1)

    cross, far, near = {}, {}, {}

    def send_tokens(n):
        wo = 2 * z + (1 - lo)
        TA[n, 0:128] = tokens(562, wo, n)
        TA[n, 128:256] = tokens(850, wo, n)
        ta, tb = TH.at[lo, n, pl.ds(al(a0, 128), 128)], TH.at[lo, n, pl.ds(al(b0, 128), 128)]
        cross[n] = []
        for xx in (xp, xm):
            cross[n] += [
                st.go(TA.at[n, pl.ds(0, 128)], ta, dev(xx, y, z, c)),
                st.go(TA.at[n, pl.ds(128, 128)], tb, dev(xx, y, z, c)),
            ]
        TH[lo, n, pl.ds(al(s * 256, 256), 128)] = tokens(18, p, n)
        TH[lo, n, pl.ds(al(s * 256 + 128, 128), 128)] = tokens(274, p, n)
        far[n] = same(TH.at[lo, n, blk], dev(x2, y, z, c))
        near[n] = [same(TH.at[lo, n, blk], sib)]

    def pass_cross(n):
        for cp in cross[n]:
            cp.wait_recv()
        near[n].append(same(TH.at[1 - lo, n, blk], sib))
        near[n].append(same(TH.at[1 - lo, n, blk2], sib))

    def pass_far(n):
        far[n].wait_recv()
        near[n].append(same(TH.at[lo, n, blk2], sib))

    def norm(block):
        at = pl.ds(al(block * 256, 256), 256)
        ms = 0.0
        for a in range(2):
            for n in range(3):
                h = TH[a, n, at].astype(F32)
                ms = ms + jnp.sum(h * h, axis=1, keepdims=True)
        r = lax.rsqrt(ms / D + 1e-05)
        for a in range(2):
            for n in range(3):
                lanes = slice(a * HALF + n * 256, a * HALF + n * 256 + 256)
                NM[at, lanes] = (TH[a, n, at].astype(F32) * r * VEC[1:2, lanes]).astype(BF)

    def start_gq():
        wait_swap()
        gq.p0()

    def start_go():
        for cp in swap_o:
            cp.wait_recv()
        go.p0()

    sq = []

    def finish_gq():
        gq.p5((0, -1, 1, 2))
        other = pl.ds(al(2 * (1 - c), 2), 2)
        sq.append(same(AW.at[:, other, :, :, cols], sib))

    def norms(k):
        if k == 0:
            norm(s)
            norm(s2)
            hs = {(a, n): TH[a, n, blk] for a in range(2) for n in range(3)}
            TOK[...] = jnp.concatenate(
                [hs[a, n][:, b * 64:(b + 1) * 64] for b in range(4) for a in range(2) for n in range(3)], axis=1
            )
        else:
            for n in range(3):
                for cp in near[n]:
                    cp.wait_recv()
            norm(2 * hi + 1 - c)
            norm(2 * (1 - hi) + 1 - c)

    heads = pl.ds(al(2 * c, 2), 2)

    def keys_values(k):
        if k == 0:
            sq[0].wait_recv()
        w = AW[1:3, heads].reshape(4 * HEAD, D)
        for b in (s, s2) if k == 0 else (2 * hi + 1 - c, 2 * (1 - hi) + 1 - c):
            at = pl.ds(al(b * 256, 256), 256)
            res = nt(NM[at], w).astype(BF)
            for h in range(4):
                QH[1 + h // 2, h % 2, at] = res[:, h * HEAD:(h + 1) * HEAD]

    scale = math.log2(math.e) / math.sqrt(HEAD)
    lop = lax.rem(lo + hi, 2)
    my_cols = pl.ds(al(c * 384, 128), 384)
    back = []
    dests = [(1 - hi, c, x2, c), (1 - hi, 1 - c, x2, 1 - c), (hi, 1 - c, x, 1 - c), (hi, c, None, None)]

    def attend(d):
        dhi, dc, dx, dcc = dests[d]
        at = pl.ds(al((2 * dhi + dc) * 256, 256), 256)
        res = nt(NM[at], AW[0, heads].reshape(2 * HEAD, D)).astype(BF)
        for h in range(2):
            QH[0, h, at] = res[:, h * HEAD:(h + 1) * HEAD]
        for h in range(2):
            sc = nt(QH[0, h, at], QH[1, h])
            e = jnp.exp2((sc - jnp.max(sc, axis=1, keepdims=True)) * scale)
            inv = 1.0 / jnp.sum(e, axis=1, keepdims=True)
            AO[d, h] = (nn(e.astype(BF), QH[2, h]) * inv).astype(BF)
        both = jnp.concatenate([AO[d, 0], AO[d, 1]], axis=1)
        if dx is None:
            AT[lop, :, my_cols] = both
        else:
            BO[d] = both
            back.append(st.go(BO.at[d], AT.at[lop, :, my_cols], dev(dx, y, z, dcc)))

    def project(k):
        if k == 0:
            for cp in to_core:
                cp.wait_recv()
            back[2].wait_recv()

            def body(n, carry):
                at = pl.ds(al(n * 256, 256), 256)
                MX[:, at] = TOK[:, at].astype(F32) + nn(AT[lop], OW[lop, :, :, :, at].reshape(HALF, 256))
                return carry
        else:
            for cp in back[:2]:
                cp.wait_recv()

            def body(n, carry):
                at = pl.ds(al(n * 256, 256), 256)
                mixed = nn(AT[1 - lop], OW[1 - lop, :, :, :, at].reshape(HALF, 256))
                seq_out[:, at] = (MX[:, at] + mixed).astype(BF)
                return carry
        lax.fori_loop(0, 6, body, 0)

    done = {
        "Z": lambda k: k == 0 or start_zA(k), "A": pass_zA, "B": pass_zB, "Y": pass_yA, "C": pass_yC,
        "F": lambda k: ready_features(), "T": conv_tap, "S": send_tokens, "X": pass_cross, "W": pass_far,
        "g0": start_gq, "g+": lambda: gq.p1(1), "g-": lambda: gq.p1(-1), "gb": gq.p2, "gP": gq.second_pass,
        "gQ": finish_gq,
        "o0": start_go, "o+": lambda: go.p1(1), "o-": lambda: go.p1(-1), "ob": go.p2, "oP": go.second_pass,
        "oQ": lambda j: go.to_sib((j,)),
        "N": norms, "V": keys_values, "D": attend, "O": project,
    }
    for what, *at in ORDER:
        if what == "O" and at[0] == 1:
            sent = len(st.all) - 3
            for cp in st.all[:sent]:
                cp.wait_send()
        done[what](*at)

    rows = jnp.sum(seq_out[...].astype(F32).reshape(16, POOL, D), axis=1) * (1.0 / POOL)
    unit = (rows * lax.rsqrt(jnp.mean(rows * rows, axis=1, keepdims=True) + 1e-05)).astype(BF)
    LW[...] = nn(unit, lw[...]).astype(BF)
    RW[...] = nn(unit, rw[...]).astype(BF).astype(F32)

    lefts = [st.go(LW, L.at[p], (s, lax.rem(p + d, 8), y)) for d in range(1, 8)]
    L[p] = LW[...]

    def right_copy(q, half):
        return pltpu.make_async_remote_copy(
            src_ref=RW.at[pl.ds(8 * half, 8)], dst_ref=R.at[p], send_sem=ssr.at[2 * q + half],
            recv_sem=rsr.at[p], device_id=(q, 2 * s + half, y), device_id_type=MESH,
        )

    for q in range(4):
        for half in range(2):
            me = jnp.logical_and(p == 2 * s + half, q == s)

            @pl.when(jnp.logical_not(me))
            def _(q=q, half=half):
                right_copy(q, half).start()

            @pl.when(me)
            def _(half=half):
                R[p] = RW[8 * half:8 * half + 8, :]

    for cp in lefts:
        cp.wait_recv()
    for w in range(8):
        @pl.when(jnp.logical_not(jnp.logical_and(inside, p == w)))
        def _(w=w):
            pltpu.make_async_remote_copy(
                src_ref=RW.at[pl.ds(0, 8)], dst_ref=R.at[w], send_sem=ssr.at[0],
                recv_sem=rsr.at[w], device_id=(s, p, y), device_id_type=MESH,
            ).wait_recv()

    outer = L[...].astype(F32)[:, :, None, :] * R[...][:, None, :, :]
    pair_out[...] = nn(outer.reshape(1024, 128).astype(BF), mix[...]).astype(BF)

    for cp in st.all[sent:]:
        cp.wait_send()
    swap_q[0].wait_send()
    for q in range(4):
        for half in range(2):
            @pl.when(jnp.logical_not(jnp.logical_and(p == 2 * s + half, q == s)))
            def _(q=q, half=half):
                right_copy(q, half).wait_send()


def local(
    features, conv_weight, conv_bias, species_table, species_id, norm_gain,
    qkv_weight, out_weight, left_weight, right_weight, mix_weight,
):
    any_ = pl.BlockSpec(memory_space=pl.ANY)
    vm = pl.BlockSpec(memory_space=pltpu.VMEM)
    seq_out, pair_map = pl.pallas_call(
        main_kernel,
        out_shape=(jax.ShapeDtypeStruct((256, D), BF), jax.ShapeDtypeStruct((1024, 128), BF)),
        in_specs=[any_] * 4 + [vm] * 7,
        out_specs=(vm, vm),
        scratch_shapes=[
            pltpu.VMEM((ROWS, D), BF),
            pltpu.VMEM((3, 5, 256, D), BF),
            pltpu.VMEM((6, ROWS + 8, 128), F32),
            pltpu.VMEM((3, 48, D), BF),
            pltpu.VMEM((3, 4, 4, 48, D), BF),
            pltpu.VMEM((2, 4, 4, 48, D), BF),
            pltpu.VMEM((2, 3, 1024, 256), BF),
            pltpu.VMEM((3, 256, 256), BF),
            pltpu.VMEM((256, D), BF),
            pltpu.VMEM((1024, D), BF),
            pltpu.VMEM((3, 2, 1024, HEAD), BF),
            pltpu.VMEM((4, 2, 256, HEAD), BF),
            pltpu.VMEM((2, 256, HALF), BF),
            pltpu.VMEM((3, 256, 384), BF),
            pltpu.VMEM((256, D), F32),
            pltpu.VMEM((4, D), F32),
            pltpu.VMEM((16, 128), BF),
            pltpu.VMEM((16, 128), F32),
            pltpu.VMEM((8, 16, 128), BF),
            pltpu.VMEM((8, 8, 128), F32),
            pltpu.SemaphoreType.DMA((N_SITES + 2,)),
            pltpu.SemaphoreType.DMA((N_SITES + 2,)),
            pltpu.SemaphoreType.DMA((7,)),
            pltpu.SemaphoreType.DMA((8,)),
            pltpu.SemaphoreType.DMA((8,)),
        ],
        compiler_params=pltpu.CompilerParams(
            collective_id=0, has_side_effects=True, vmem_limit_bytes=62 * 2**20
        ),
        name="window",
    )(
        features.reshape(512, D), conv_weight, qkv_weight, out_weight, conv_bias, norm_gain,
        species_table, species_id, left_weight, right_weight, mix_weight,
    )
    return seq_out[None, None], pair_map.reshape(1, 8, 16, 8, 128)


def solution(mesh):
    return jax.shard_map(
        local,
        mesh=mesh,
        in_specs=(
            P("dp", "pair", "seq", None),
            P(None, "pair", None),
            P(),
            P(),
            P("dp", None),
            P(),
            P(None, ("pair", "dp"), None),
            P(("pair", "dp"), None),
            P(),
            P(),
            P(),
        ),
        out_specs=(P("dp", "pair", "seq", None), P("dp", None, "seq", "pair", None)),
        check_vma=False,
    )
```
